256 devices in a mesh: inst: 32 (over x, z_lo, core), tp: 8 (over z_hi, y).
Axes of the slice: x: 4, y: 4, z: 8 (z_hi: 2, z_lo: 4; z = z_hi * 4 + z_lo), core: 2. Of those that a mesh axis runs over, the one named last changes fastest.
Arguments:
- queries: bfloat16 [2048, 2, 8192], P('inst', None, 'tp'), may hold values from -6 to 6
- new_kv: bfloat16 [2048, 2, 2048], P('inst', None, 'tp'), may hold values from -6 to 6
- kv_cache: bfloat16 [16384, 16, 2048], P('inst', None, 'tp'), may hold values from -6 to 6
- block_table: int32 [2048, 8], P('inst'), may hold values from 0 to 511, as said below
- lengths: int32 [2048], P('inst'), may hold values from 1 to 128, as said below
- mig_rows: int32 [768], P('inst'), may hold values from 0 to 63, as said below
- mig_target: int32 [768], P('inst'), may hold values from 0 to 31, as said below
- dirty_hidden: bfloat16 [768, 16, 8192], P('inst', None, 'tp'), may hold values from -60 to 60
- norm_gain: bfloat16 [8192], replicated, may hold values from 0.25 to 1.75
- kv_weight: bfloat16 [8192, 2048], P(None, 'tp'), may hold values from -0.0625 to 0.0625
Outputs:
- decoded: bfloat16 [2048, 2, 8192], P('inst', None, 'tp')
- mig_kv: bfloat16 [8192, 16, 2048], P('inst', None, 'tp')
The draws below stay inside these ranges and needn't reach their ends.
Inputs may be any that keep to these rules, and one draw needn't show every extreme that they name: `lengths`: every instance has a request of exactly 128 tokens. `block_table`: the rows of one instance use distinct pages of its own pool. `mig_rows`: the 24 rows of one instance are distinct. `mig_target`: a target differs from its source; slots 2c and 2c + 1 of an instance share a target and the pairs of one instance go to distinct targets, so at most 2 requests of one instance go to one target, and their pages together are at most 8; some instance receives exactly 8 pages from every other instance.
All inputs are finite; a program needn't handle non-finite values.
Results may differ from the reference program's by a relative error of at most 0.0049.
Values may be sent and summed in bfloat16 or wider, within the bound.
No kernel may reach another device: no remote copies, remote signals or barrier semaphores. Data moves between devices by JAX's collectives and lax.ppermute only.
A program may use at most 128 MiB of HBM per device.

```python
import math
from functools import partial
import jax
import jax.numpy as jnp
from jax import lax

D = 8192
QH = 64
KVH = 8
HD = 128
PAGE = 16
MAXP = 8
MIG = 24
ROWS = 64
PAGES = 512
N_INST = 32


def migration_plan(key):
    sub_keys = jax.random.split(key, 9)
    pair_count = MIG // 2
    instance_ids = jnp.arange(N_INST, dtype=jnp.int32)
    row_orders = jax.vmap(partial(jax.random.permutation, x=ROWS))(jax.random.split(sub_keys[0], N_INST)).astype(jnp.int32)
    movers = row_orders[:, :MIG]
    hottest = jax.random.randint(sub_keys[1], (), 0, N_INST)
    target_orders = jax.vmap(partial(jax.random.permutation, x=N_INST))(jax.random.split(sub_keys[2], N_INST)).astype(jnp.int32)
    barred = (target_orders == instance_ids[:, None]) | (target_orders == hottest)
    ranking = barred.astype(jnp.int32) * N_INST + jnp.arange(N_INST, dtype=jnp.int32)[None, :]
    picks = jnp.argsort(ranking, axis=1, stable=True)[:, :pair_count]
    leading = jnp.take_along_axis(target_orders, picks, axis=1)
    hot_goal = jnp.where(instance_ids == hottest, leading[:, 0], hottest)
    leading = leading.at[:, 0].set(hot_goal)
    targets = jnp.stack([leading, leading], axis=2).reshape(N_INST, MIG)
    first_pages = jax.random.randint(sub_keys[4], (N_INST, pair_count), 1, MAXP)
    spare = jax.random.randint(sub_keys[5], (N_INST, pair_count), 0, 1 << 20)
    paired = 1 + spare % (MAXP - first_pages)
    paired = paired.at[:, 0].set(MAXP - first_pages[:, 0])
    page_counts = jnp.stack([first_pages, paired], axis=2).reshape(N_INST, MIG)
    tails = jax.random.randint(sub_keys[7], (N_INST, MIG), 1, PAGE + 1)
    row_lengths = jax.random.randint(sub_keys[8], (N_INST, ROWS), 1, MAXP * PAGE + 1)
    row_lengths = row_lengths.at[instance_ids[:, None], movers].set((page_counts - 1) * PAGE + tails)
    row_lengths = row_lengths.at[instance_ids, row_orders[:, MIG]].set(MAXP * PAGE)
    return (row_lengths.reshape(-1).astype(jnp.int32), movers.reshape(-1).astype(jnp.int32), targets.reshape(-1).astype(jnp.int32))


def draw_lengths(key, part):
    plan = migration_plan(key)
    return plan[0]


def draw_mig_rows(key, part):
    plan = migration_plan(key)
    return plan[1]


def draw_mig_target(key, part):
    plan = migration_plan(key)
    return plan[2]


def draw_block_table(key, part):
    own_key = jax.random.fold_in(key, 11)
    orders = jax.vmap(partial(jax.random.permutation, x=PAGES))(jax.random.split(own_key, N_INST))
    return orders.reshape(N_INST * ROWS, MAXP).astype(jnp.int32)


def draw_queries(key, part):
    own_key = jax.random.fold_in(key, 31)
    row_total = N_INST * ROWS
    sample = jnp.clip(jax.random.normal(own_key, (row_total, 2, QH * HD), jnp.float32), -6.0, 6.0)
    return sample.astype(jnp.bfloat16)


def draw_new_kv(key, part):
    own_key = jax.random.fold_in(key, 37)
    row_total = N_INST * ROWS
    sample = jnp.clip(jax.random.normal(own_key, (row_total, 2, KVH, 2, HD), jnp.float32), -6.0, 6.0)
    return sample.reshape(row_total, 2, KVH * 2 * HD).astype(jnp.bfloat16)


def draw_dirty_hidden(key, part):
    own_key = jax.random.fold_in(key, 41)
    sub_keys = jax.random.split(own_key, 3)
    item_total = N_INST * MIG
    row_scale = jnp.exp(jax.random.uniform(sub_keys[1], (item_total, PAGE, 1), jnp.float32, 0.0, math.log(10.0)))
    column_scale = jnp.exp(jax.random.uniform(sub_keys[2], (1, 1, D), jnp.float32, math.log(0.3), math.log(3.0)))
    base = jnp.clip(jax.random.normal(sub_keys[0], (item_total, PAGE, D), jnp.float32), -2.0, 2.0)
    return jnp.clip(base * row_scale * column_scale, -60.0, 60.0).astype(jnp.bfloat16)


def level_of(key, extent, shards, least, high):
    def one(axis_at, shards_of):
        heights = jax.random.uniform(jax.random.fold_in(jax.random.fold_in(key, 6), axis_at), (shards_of,), jnp.float32, least / len(shards), high / len(shards))
        return jnp.repeat(jnp.exp(heights), extent[axis_at] // shards_of).reshape((-1,) + (1,) * (len(extent) - axis_at - 1))

    factor_of = one(*shards[0])
    for cut in shards[1:]:
        factor_of = factor_of * one(*cut)
    return factor_of


def scatter_about(stream_key, shape, spread, bound, cuts=(), kind=jnp.bfloat16):
    factor_of = level_of(stream_key, shape, cuts, -0.22, 0.18) if cuts else 1.0
    array = jax.random.normal(stream_key, shape, jnp.float32) * spread * factor_of
    return jnp.minimum(jnp.maximum(array, -bound), bound).astype(kind)


def setup_inputs(seed: int = 0) -> dict:
    key_of = jax.random.split(jax.random.key(seed), 11)
    queries = draw_queries(jax.random.fold_in(key_of[10], 71), 0)
    new_kv = draw_new_kv(jax.random.fold_in(key_of[10], 71), 0)
    kv_cache = scatter_about(key_of[2], (N_INST * PAGES, PAGE, KVH * 2 * HD), 1.0, 6.0, ((0, 32), (2, 8)))
    block_table = draw_block_table(jax.random.fold_in(key_of[10], 71), 0)
    lengths = draw_lengths(jax.random.fold_in(key_of[10], 71), 0)
    mig_rows = draw_mig_rows(jax.random.fold_in(key_of[10], 71), 0)
    mig_target = draw_mig_target(jax.random.fold_in(key_of[10], 71), 0)
    dirty_hidden = draw_dirty_hidden(jax.random.fold_in(key_of[10], 71), 0)
    norm_gain = jnp.clip(1.0 + 0.15 * jax.random.normal(key_of[8], (D,), jnp.float32), 0.25, 1.75).astype(jnp.bfloat16)
    kv_weight = scatter_about(key_of[9], (D, KVH * 2 * HD), D ** -0.5, 0.0625, ((1, 8),))
    return {"queries": queries, "new_kv": new_kv, "kv_cache": kv_cache, "block_table": block_table, "lengths": lengths, "mig_rows": mig_rows, "mig_target": mig_target, "dirty_hidden": dirty_hidden, "norm_gain": norm_gain, "kv_weight": kv_weight}


def rotate_keys(key_part, positions):
    half_dim = key_part.shape[-1] // 2
    frequency = jnp.exp(jnp.arange(half_dim, dtype=jnp.float32) * (-2.0 * math.log(500000.0) / key_part.shape[-1]))
    angles = positions.astype(jnp.float32)[..., None, None] * frequency
    cosine = jnp.cos(angles)
    sine_part = jnp.sin(angles)
    first_half = key_part[..., :half_dim]
    second = key_part[..., half_dim:]
    return jnp.concatenate([first_half * cosine - second * sine_part, second * cosine + first_half * sine_part], axis=-1)

def refill(hidden, gain_vec, weight, first_pos, valid_count):
    item_count = hidden.shape[0]
    page_len = hidden.shape[1]
    head_count = weight.shape[1] // (2 * HD)
    states = hidden.astype(jnp.float32)
    mean_square = lax.optimization_barrier(jnp.mean(states * states, axis=-1, keepdims=True))
    normed = (states * lax.rsqrt(mean_square + 1e-05) * gain_vec.astype(jnp.float32)).astype(jnp.bfloat16)
    projected = jnp.dot(normed.reshape(item_count * page_len, -1), weight, preferred_element_type=jnp.float32)
    projected = projected.reshape(item_count, page_len, head_count, 2, HD)
    offsets = jnp.arange(page_len, dtype=jnp.int32)
    positions = first_pos[:, None] + offsets[None, :]
    rotated = rotate_keys(projected[:, :, :, 0, :], positions)
    merged = jnp.stack([rotated, projected[:, :, :, 1, :]], axis=3).reshape(item_count, page_len, head_count * 2 * HD)
    keep_mask = offsets[None, :] < valid_count[:, None]
    return jnp.where(keep_mask[:, :, None], merged, 0.0).astype(jnp.bfloat16)

def attend(queries, new_kv, gathered, row_lengths):
    row_count = queries.shape[0]
    head_count = gathered.shape[-1] // (2 * HD)
    group_size = queries.shape[-1] // (HD * head_count)
    span_len = gathered.shape[1]
    stored_tokens = gathered.reshape(row_count, span_len, head_count, 2, HD).astype(jnp.float32)
    query_heads = queries.reshape(row_count, 2, head_count, group_size, HD).astype(jnp.float32)
    fresh_tokens = new_kv.reshape(row_count, 2, head_count, 2, HD).astype(jnp.float32)
    score_scale = 1.0 / math.sqrt(HD)
    cached_scores = jnp.einsum('rsghd,rtgd->rsght', query_heads, stored_tokens[:, :, :, 0]) * score_scale
    own_scores = jnp.einsum('rsghd,rugd->rsghu', query_heads, fresh_tokens[:, :, :, 0]) * score_scale
    live_tokens = jnp.arange(span_len, dtype=jnp.int32)[None, :] < row_lengths[:, None]
    cached_scores = jnp.where(live_tokens[:, None, None, None, :], cached_scores, -jnp.inf)
    step_index = jnp.arange(2, dtype=jnp.int32)
    visible = step_index[None, :] <= step_index[:, None]
    own_scores = jnp.where(visible[None, :, None, None, :], own_scores, -jnp.inf)
    scores = jnp.concatenate([cached_scores, own_scores], axis=-1)
    row_max = lax.optimization_barrier(jnp.max(scores, axis=-1, keepdims=True))
    raised = jnp.exp(scores - row_max)
    weights = (raised / lax.optimization_barrier(jnp.sum(raised, axis=-1, keepdims=True))).astype(jnp.bfloat16)
    mixture = jnp.einsum('rsght,rtgd->rsghd', weights[..., :span_len].astype(jnp.float32), stored_tokens[:, :, :, 1])
    mixture = mixture + jnp.einsum('rsghu,rugd->rsghd', weights[..., span_len:].astype(jnp.float32), fresh_tokens[:, :, :, 1])
    return mixture.reshape(row_count, 2, head_count * group_size * HD).astype(jnp.bfloat16)

def reference(queries, new_kv, kv_cache, block_table, lengths, mig_rows, mig_target, dirty_hidden, norm_gain, kv_weight):
    lane_width = kv_cache.shape[-1]
    pool_pages = kv_cache.reshape(N_INST, PAGES, PAGE, lane_width)
    tables = block_table.reshape(N_INST, ROWS, MAXP)
    row_lengths = lengths.reshape(N_INST, ROWS)

    def one_instance(inputs):
        query_rows, fresh_rows, pool_one, table_one, length_one = inputs
        gathered = pool_one[table_one].reshape(ROWS, MAXP * PAGE, lane_width)
        return attend(query_rows, fresh_rows, gathered, length_one)
    decoded = lax.map(one_instance, (queries.reshape(N_INST, ROWS, 2, -1), new_kv.reshape(N_INST, ROWS, 2, -1), pool_pages, tables, row_lengths))
    decoded = decoded.reshape(N_INST * ROWS, 2, -1)
    movers = mig_rows.reshape(N_INST, MIG)
    target_ids = mig_target.reshape(N_INST, MIG)
    mig_len = jnp.take_along_axis(row_lengths, movers, axis=1)
    mig_pages = (mig_len + PAGE - 1) // PAGE
    first_pos = ((mig_pages - 1) * PAGE).reshape(-1)
    valid_count = (mig_len - (mig_pages - 1) * PAGE).reshape(-1)
    fresh_pages = refill(dirty_hidden, norm_gain, kv_weight, first_pos, valid_count).reshape(N_INST, MIG, PAGE, lane_width)
    held_pages = jnp.take_along_axis(tables, movers[:, :, None], axis=1)
    source_ids = jnp.arange(N_INST, dtype=jnp.int32)[:, None, None]
    stored_pages = pool_pages[source_ids, held_pages]
    page_slot = jnp.arange(MAXP, dtype=jnp.int32)[None, None, :]
    is_last = page_slot == (mig_pages - 1)[:, :, None]
    outgoing_pages = jnp.where(is_last[..., None, None], fresh_pages[:, :, None], stored_pages)
    in_use = page_slot < mig_pages[:, :, None]
    slot_order = jnp.arange(MIG, dtype=jnp.int32)
    earlier = (slot_order[None, :] < slot_order[:, None])[None]
    same_goal = target_ids[:, :, None] == target_ids[:, None, :]
    offset = lax.optimization_barrier(jnp.sum(jnp.where(same_goal & earlier, mig_pages[:, None, :], 0), axis=2))
    target_place = (target_ids[:, :, None] * N_INST + source_ids) * MAXP + offset[:, :, None] + page_slot
    target_place = jnp.where(in_use, target_place, N_INST * N_INST * MAXP).astype(jnp.int32)
    mig_kv = jnp.zeros((N_INST * N_INST * MAXP, PAGE, lane_width), jnp.bfloat16)
    mig_kv = mig_kv.at[target_place.reshape(-1)].set(outgoing_pages.reshape(-1, PAGE, lane_width), mode='drop')
    return (decoded, mig_kv)
```

```python
import functools
import math

import jax
import jax.numpy as jnp
from jax import lax
from jax.experimental import pallas as pl
from jax.experimental.pallas import tpu as pltpu
from jax.sharding import PartitionSpec as P

HD = 128
PAGE = 16
MAXP = 8
MIG = 24
PAIRS = MIG // 2
STORED = MAXP - 2
NX, NZL, NCORE, NZH, NY = 4, 4, 2, 2, 4
TP = NZH * NY
AXES = ("inst", "tp")
VMEM_LIMIT = 40 * 1024 * 1024
F32 = jnp.float32
BF16 = jnp.bfloat16


def index_of(x, zl, core, zh, y):
    return (((x * NZL + zl) * NCORE) + core) * TP + zh * NY + y


def moves(dx=0, dcore=0, dzh=0, dy=0):
    pairs = []
    for x in range(NX):
        for zl in range(NZL):
            for core in range(NCORE):
                for zh in range(NZH):
                    for y in range(NY):
                        pairs.append(
                            (
                                index_of(x, zl, core, zh, y),
                                index_of(
                                    (x + dx) % NX,
                                    zl,
                                    (core + dcore) % NCORE,
                                    (zh + dzh) % NZH,
                                    (y + dy) % NY,
                                ),
                            )
                        )
    return pairs


def send(value, **by):
    return lax.ppermute(value, AXES, moves(**by))


def params(**more):
    return pltpu.CompilerParams(vmem_limit_bytes=VMEM_LIMIT, **more)


SMEM = pl.BlockSpec(memory_space=pltpu.SMEM)
VMEM = pl.BlockSpec(memory_space=pltpu.VMEM)
ANY = pl.BlockSpec(memory_space=pl.ANY)


def pack_kernel(rows_ref, target_ref, len_ref, table_ref, cache_ref, out_ref, sems):
    def copy_of(c, m):
        first = rows_ref[2 * c]
        second = rows_ref[2 * c + 1]
        front = (len_ref[first] + PAGE - 1) // PAGE - 1
        in_front = m < front
        row = jnp.where(in_front, first, second)
        slot = jnp.where(in_front, m, jnp.minimum(m - front, MAXP - 1))
        page = table_ref[row, slot]
        return pltpu.make_async_copy(
            cache_ref.at[page], out_ref.at[target_ref[2 * c] * STORED + m], sems.at[c * STORED + m]
        )

    for c in range(PAIRS):
        for m in range(STORED):
            copy_of(c, m).start()
    for c in range(PAIRS):
        for m in range(STORED):
            copy_of(c, m).wait()


def pack(rows, target, lengths, table, cache, members):
    lanes = cache.shape[-1]
    return pl.pallas_call(
        pack_kernel,
        out_shape=jax.ShapeDtypeStruct((members * STORED, PAGE, lanes), cache.dtype),
        in_specs=[SMEM, SMEM, SMEM, SMEM, ANY],
        out_specs=ANY,
        scratch_shapes=[pltpu.SemaphoreType.DMA((PAIRS * STORED,))],
        compiler_params=params(),
        cost_estimate=pl.CostEstimate(flops=0, bytes_accessed=8 * 1024 * 1024, transcendentals=0),
        name="pack",
    )(rows, target, lengths, table, cache)


def attend_kernel(table_ref, len_ref, q_ref, new_ref, cache_ref, out_ref):
    row_count, heads, _ = q_ref.shape
    span = MAXP * PAGE + PAGE
    scale = 1.0 / math.sqrt(HD)
    column = lax.broadcasted_iota(jnp.int32, (heads, span), 1)
    step = lax.broadcasted_iota(jnp.int32, (heads, span), 0) // (heads // 2)
    own = (column >= MAXP * PAGE) & (column - MAXP * PAGE <= step)

    def one(r):
        parts = [cache_ref[table_ref[r, b]] for b in range(MAXP)] + [new_ref[r]]
        tokens = jnp.concatenate(parts, axis=0)
        scores = lax.dot_general(
            q_ref[r], tokens[:, :HD], (((1,), (1,)), ((), ())), preferred_element_type=F32
        )
        seen = (column < len_ref[r]) | own
        scores = jnp.where(seen, scores * scale, -jnp.inf)
        raised = jnp.exp(scores - jnp.max(scores, axis=-1, keepdims=True))
        weights = (raised / jnp.sum(raised, axis=-1, keepdims=True)).astype(BF16)
        out_ref[r] = jnp.dot(weights, tokens[:, HD:], preferred_element_type=F32).astype(BF16)

    unroll = 4

    def body(i, carry):
        for u in range(unroll):
            one(i * unroll + u)
        return carry

    lax.fori_loop(0, row_count // unroll, body, 0)


def attend(queries, new_kv, cache, table, lengths):
    row_count = queries.shape[0]
    heads = queries.shape[-1] // HD
    q = queries.reshape(row_count, 2 * heads, HD)
    fresh = jnp.pad(new_kv, ((0, 0), (0, PAGE - 2), (0, 0)))
    out = pl.pallas_call(
        attend_kernel,
        out_shape=jax.ShapeDtypeStruct((row_count, 2 * heads, HD), BF16),
        in_specs=[SMEM, SMEM, VMEM, VMEM, VMEM],
        out_specs=VMEM,
        compiler_params=params(),
        cost_estimate=pl.CostEstimate(
            flops=64 * 16 * 144 * 128 * 4, bytes_accessed=32 * 1024 * 1024, transcendentals=0
        ),
        name="attend",
    )(table, lengths, q, fresh, cache)
    return out.reshape(row_count, 2, heads * HD)


def project_kernel(count, has_acc, place_ref, gain_ref, own_ref, mine_ref, other_ref, *refs):
    blocks = refs[:count]
    refs = refs[count:]
    if has_acc:
        acc_own_ref, acc_oth_ref = refs[:2]
        refs = refs[2:]
    out_own_ref, out_oth_ref, x_ref = refs
    core = place_ref[0]
    depth = blocks[0].shape[1]
    half = depth // 2
    for i, block in enumerate(blocks):
        feature = place_ref[1 + 3 * i]
        near = place_ref[2 + 3 * i]
        gain = gain_ref[pl.ds(feature, 1), :]
        x_ref[...] = (block[...].astype(F32) * gain).astype(BF16)
        part_own = jnp.dot(
            x_ref[...],
            own_ref[pl.ds(pl.multiple_of(feature * depth, depth), depth), :],
            preferred_element_type=F32,
        )
        rows = pl.ds(pl.multiple_of(near * half, half), half)
        part_oth = jnp.dot(
            x_ref[:, pl.ds(pl.multiple_of(core * half, half), half)],
            mine_ref[rows, :],
            preferred_element_type=F32,
        ) + jnp.dot(
            x_ref[:, pl.ds(pl.multiple_of((1 - core) * half, half), half)],
            other_ref[rows, :],
            preferred_element_type=F32,
        )
        if i == 0:
            if has_acc:
                part_own = part_own + acc_own_ref[...]
                part_oth = part_oth + acc_oth_ref[...]
            sum_own, sum_oth = part_own, part_oth
        else:
            sum_own, sum_oth = sum_own + part_own, sum_oth + part_oth
    out_own_ref[...] = sum_own
    out_oth_ref[...] = sum_oth.astype(out_oth_ref.dtype)


def project(place, gain, own, mine, other, blocks, acc, oth_dtype):
    tokens, depth = blocks[0].shape
    width = own.shape[1]
    shape = (tokens, width)
    args = list(blocks) + (list(acc) if acc else [])
    return pl.pallas_call(
        functools.partial(project_kernel, len(blocks), bool(acc)),
        out_shape=(jax.ShapeDtypeStruct(shape, F32), jax.ShapeDtypeStruct(shape, oth_dtype)),
        in_specs=[SMEM] + [VMEM] * (4 + len(args)),
        out_specs=(VMEM, VMEM),
        scratch_shapes=[pltpu.VMEM((tokens, depth), BF16)],
        compiler_params=params(),
        cost_estimate=pl.CostEstimate(
            flops=len(blocks) * tokens * depth * width * 4,
            bytes_accessed=8 * 1024 * 1024,
            transcendentals=0,
        ),
        name="project",
    )(place, gain, own, mine, other, *args)


def combine_kernel(target_ref, own_ref, got_ref, cos_ref, sin_ref, inv_ref, out_ref):
    total = own_ref[...] + got_ref[...].astype(F32)
    keys = total[:, :HD]
    turned = keys * cos_ref[...] + pltpu.roll(keys, HD // 2, 1) * sin_ref[...]
    page_rows = jnp.concatenate([turned, total[:, HD:] * inv_ref[...]], axis=1).astype(BF16)
    for k in range(MIG):
        out_ref[target_ref[k] * 2 + k % 2] = page_rows[k * PAGE : (k + 1) * PAGE]


def combine(target, own, got, cos_t, sin_t, inv_t, members):
    return pl.pallas_call(
        combine_kernel,
        out_shape=jax.ShapeDtypeStruct((members * 2, PAGE, own.shape[1]), BF16),
        in_specs=[SMEM] + [VMEM] * 5,
        out_specs=VMEM,
        compiler_params=params(),
        name="combine",
    )(target, own, got, cos_t, sin_t, inv_t)


def assemble_kernel(sources, counts_ref, stored_ref, dirty_ref, out_ref):
    base = pl.program_id(0) * sources

    def one(s, carry):
        first = counts_ref[base + s, 0]
        second = counts_ref[base + s, 1]
        for m in range(MAXP):
            behind = (m >= first).astype(jnp.int32)
            index = jnp.clip(m - behind, 0, STORED - 1)
            kept = stored_ref[s * STORED + index]
            made = dirty_ref[s * 2 + behind]
            is_made = (m == first - 1) | (m == first + second - 1)
            page = jnp.where(is_made, made, kept)
            out_ref[s * MAXP + m] = jnp.where(m < first + second, page, jnp.zeros_like(page))
        return carry

    lax.fori_loop(0, sources, one, 0)


def assemble(counts, stored, dirty, members):
    lanes = stored.shape[-1]
    steps = 4
    sources = members // steps
    return pl.pallas_call(
        functools.partial(assemble_kernel, sources),
        out_shape=jax.ShapeDtypeStruct((members * MAXP, PAGE, lanes), stored.dtype),
        grid=(steps,),
        in_specs=[
            SMEM,
            pl.BlockSpec((sources * STORED, PAGE, lanes), lambda i: (i, 0, 0)),
            pl.BlockSpec((sources * 2, PAGE, lanes), lambda i: (i, 0, 0)),
        ],
        out_specs=pl.BlockSpec((sources * MAXP, PAGE, lanes), lambda i: (i, 0, 0)),
        compiler_params=params(),
        name="assemble",
    )(counts, stored, dirty)


def exchange(pages, members, each):
    lanes = pages.shape[-1]
    moved = lax.all_to_all(
        pages.reshape(members, each * PAGE, lanes), "inst", split_axis=0, concat_axis=0, tiled=True
    )
    return moved.reshape(members * each, PAGE, lanes)


def per_device(
    queries,
    new_kv,
    kv_cache,
    block_table,
    lengths,
    mig_rows,
    mig_target,
    dirty_hidden,
    norm_gain,
    kv_weight,
):
    members = lax.axis_size("inst")
    inst = lax.axis_index("inst")
    tp = lax.axis_index("tp")
    x_at, core = inst // (NZL * NCORE), inst % NCORE
    zh, y_at = tp // NY, tp % NY
    tokens = MIG * PAGE
    depth = dirty_hidden.shape[-1]
    features = depth * TP
    half_features = depth * NY

    hidden = dirty_hidden.reshape(tokens, depth)
    from_below = send(hidden, dy=1)
    from_above = send(hidden, dy=-1)
    from_across = send(hidden, dy=2)

    slice_rows = half_features // (NX * NCORE)
    begin = (1 - zh) * half_features + (x_at * NCORE + core) * slice_rows
    outgoing_slice = lax.dynamic_slice_in_dim(kv_weight, begin, slice_rows, axis=0)
    slice_here = send(outgoing_slice, dzh=1)
    slices = jnp.concatenate(
        [slice_here] + [send(slice_here, dx=-d) for d in range(1, NX)], axis=0
    )
    other_slices = send(slices, dcore=1)

    row_count = queries.shape[0]
    picked = mig_rows[:, None] == jnp.arange(row_count, dtype=jnp.int32)[None, :]
    mig_len = jnp.sum(jnp.where(picked, lengths[None, :], 0), axis=1)
    mig_pages = (mig_len + PAGE - 1) // PAGE
    notes = lax.all_gather(jnp.stack([mig_target, mig_pages]), "inst", axis=0)
    aimed_here = notes[:, 0] == inst
    counts = jnp.sum(
        jnp.where(aimed_here, notes[:, 1], 0).reshape(members, PAIRS, 2), axis=1
    )

    stored = exchange(
        pack(mig_rows, mig_target, lengths, block_table, kv_cache, members), members, STORED
    )

    squares = jnp.sum(jnp.square(hidden.astype(F32)), axis=1)
    squares = lax.psum(squares, "tp")
    inv = lax.rsqrt(squares / features + 1e-05)
    offsets = jnp.arange(PAGE, dtype=jnp.int32)
    positions = ((mig_pages - 1) * PAGE)[:, None] + offsets[None, :]
    keep = (positions < mig_len[:, None]).reshape(tokens)
    inv = jnp.where(keep, inv, 0.0)[:, None]
    half_dim = HD // 2
    frequency = jnp.exp(
        jnp.arange(half_dim, dtype=F32) * (-2.0 * math.log(500000.0) / HD)
    )
    angles = positions.reshape(tokens).astype(F32)[:, None] * frequency[None, :]
    cosine = jnp.cos(angles) * inv
    sine = jnp.sin(angles) * inv
    cos_t = jnp.concatenate([cosine, cosine], axis=1)
    sin_t = jnp.concatenate([-sine, sine], axis=1)
    inv_t = jnp.broadcast_to(inv, (tokens, HD))

    decoded = attend(queries, new_kv, kv_cache, block_table, lengths)

    gain = norm_gain.astype(F32).reshape(TP, depth)

    def place_of(shifts):
        entries = [core]
        for dy in shifts:
            block = (y_at + dy) % NY
            entries += [zh * NY + block, (block - x_at) % NX, block]
        return jnp.stack(entries).astype(jnp.int32)

    acc = project(
        place_of((0, -1, 1)),
        gain,
        kv_weight,
        slices,
        other_slices,
        (hidden, from_below, from_above),
        None,
        F32,
    )
    own, outgoing = project(
        place_of((2,)), gain, kv_weight, slices, other_slices, (from_across,), acc, BF16
    )
    got = send(outgoing, dzh=1)
    dirty = exchange(
        combine(mig_target, own, got, cos_t, sin_t, inv_t, members), members, 2
    )
    return decoded, assemble(counts, stored, dirty, members)


def solution(mesh):
    return jax.shard_map(
        per_device,
        mesh=mesh,
        in_specs=(
            P("inst", None, "tp"),
            P("inst", None, "tp"),
            P("inst", None, "tp"),
            P("inst", None),
            P("inst"),
            P("inst"),
            P("inst"),
            P("inst", None, "tp"),
            P(),
            P(None, "tp"),
        ),
        out_specs=(P("inst", None, "tp"), P("inst", None, "tp")),
        check_vma=False,
    )
```

```python
import functools
import math

import jax
import jax.numpy as jnp
from jax import lax
from jax.experimental import pallas as pl
from jax.experimental.pallas import tpu as pltpu
from jax.sharding import PartitionSpec as P

HD = 128
PAGE = 16
MAXP = 8
MIG = 24
PAIRS = MIG // 2
STORED = MAXP - 2
NX, NZL, NCORE, NZH, NY = 4, 4, 2, 2, 4
TP = NZH * NY
AXES = ("inst", "tp")
F32 = jnp.float32
BF16 = jnp.bfloat16


def index_of(x, zl, core, zh, y):
    return (((x * NZL + zl) * NCORE) + core) * TP + zh * NY + y


def moves(dx=0, dcore=0, dzh=0, dy=0, zl_xor=0):
    pairs = []
    for x in range(NX):
        for zl in range(NZL):
            for core in range(NCORE):
                for zh in range(NZH):
                    for y in range(NY):
                        pairs.append(
                            (
                                index_of(x, zl, core, zh, y),
                                index_of(
                                    (x + dx) % NX,
                                    zl ^ zl_xor,
                                    (core + dcore) % NCORE,
                                    (zh + dzh) % NZH,
                                    (y + dy) % NY,
                                ),
                            )
                        )
    return pairs


def send(value, **by):
    return lax.ppermute(value, AXES, moves(**by))


def params(mebibytes):
    return pltpu.CompilerParams(vmem_limit_bytes=mebibytes * 1024 * 1024)


SMEM = pl.BlockSpec(memory_space=pltpu.SMEM)
VMEM = pl.BlockSpec(memory_space=pltpu.VMEM)
HBM = pl.BlockSpec(memory_space=pltpu.HBM)


def meta_of(table, lengths, rows, target, place):
    parts = [table.reshape(-1), lengths, rows, target, jnp.stack(place)]
    return jnp.concatenate([p.astype(jnp.int32) for p in parts])


def meta_at(row_count):
    lengths = row_count * MAXP
    rows = lengths + row_count
    target = rows + MIG
    return lengths, rows, target, target + MIG


def pack_kernel(row_count, meta_ref, cache_ref, out_ref, sems):
    len_at, rows_at, target_at, place_at = meta_at(row_count)
    x_at, core_at = meta_ref[place_at], meta_ref[place_at + 2]
    for c in range(PAIRS):
        first = meta_ref[rows_at + 2 * c]
        second = meta_ref[rows_at + 2 * c + 1]
        target = meta_ref[target_at + 2 * c]
        x, z, core = target // (NZL * NCORE), target // NCORE % NZL, target % NCORE
        far_x = (x - x_at + NX) % NX
        base = (core ^ core_at) * STORED
        front = (meta_ref[len_at + first] + PAGE - 1) // PAGE - 1
        for m in range(STORED):
            in_front = m < front
            row = jnp.where(in_front, first, second)
            slot = jnp.where(in_front, m, jnp.minimum(m - front, MAXP - 1))
            page = meta_ref[row * MAXP + slot]
            pltpu.make_async_copy(
                cache_ref.at[page], out_ref.at[z, far_x, base + m], sems.at[c * STORED + m]
            ).start()
    for i in range(PAIRS * STORED):
        pltpu.make_async_copy(cache_ref.at[0], out_ref.at[0, 0, 0], sems.at[i]).wait()


def pack(meta, row_count, cache):
    lanes = cache.shape[-1]
    return pl.pallas_call(
        functools.partial(pack_kernel, row_count),
        out_shape=jax.ShapeDtypeStruct(
            (NZL, NX, NCORE * STORED, PAGE, lanes), cache.dtype
        ),
        in_specs=[SMEM, VMEM],
        out_specs=HBM,
        scratch_shapes=[pltpu.SemaphoreType.DMA((PAIRS * STORED,))],
        compiler_params=params(10),
        cost_estimate=pl.CostEstimate(flops=0, bytes_accessed=4 * 1024 * 1024, transcendentals=0),
        name="pack",
    )(meta, cache)


def attend_kernel(start, row_total, meta_ref, q_ref, new_ref, cache_ref, out_ref):
    row_count, heads, _ = q_ref.shape
    len_at = meta_at(row_total)[0]
    group = 8
    span = MAXP * PAGE + PAGE
    scale = 1.0 / math.sqrt(HD)
    column = lax.broadcasted_iota(jnp.int32, (heads, span), 1)
    step = lax.broadcasted_iota(jnp.int32, (heads, span), 0) // (heads // 2)
    own = (column >= MAXP * PAGE) & (column - MAXP * PAGE <= step)

    def body(i, carry):
        base = i * group
        scores = []
        values = []
        for u in range(group):
            r = base + u
            at = (start + r) * MAXP
            parts = [cache_ref[meta_ref[at + b]] for b in range(MAXP)] + [new_ref[r]]
            tokens = jnp.concatenate(parts, axis=0)
            raw = lax.dot_general(
                q_ref[r], tokens[:, :HD], (((1,), (1,)), ((), ())), preferred_element_type=F32
            )
            seen = (column < meta_ref[len_at + start + r]) | own
            scores.append(jnp.where(seen, raw * scale, -jnp.inf))
            values.append(tokens[:, HD:])
        stacked = jnp.concatenate(scores, axis=0)
        raised = jnp.exp(stacked - jnp.max(stacked, axis=-1, keepdims=True))
        weights = (raised / jnp.sum(raised, axis=-1, keepdims=True)).astype(BF16)
        mixed = [
            jnp.dot(weights[u * heads : (u + 1) * heads], values[u], preferred_element_type=F32)
            for u in range(group)
        ]
        for u in range(group):
            out_ref[base + u] = mixed[u].astype(BF16)
        return carry

    lax.fori_loop(0, row_count // group, body, 0)


def attend(start, row_total, q, fresh, cache, meta):
    row_count, heads, _ = q.shape
    return pl.pallas_call(
        functools.partial(attend_kernel, start, row_total),
        out_shape=jax.ShapeDtypeStruct((row_count, heads, HD), BF16),
        in_specs=[SMEM, VMEM, VMEM, VMEM],
        out_specs=VMEM,
        compiler_params=params(14),
        cost_estimate=pl.CostEstimate(
            flops=row_count * 16 * 144 * 128 * 4,
            bytes_accessed=row_count * 512 * 1024,
            transcendentals=0,
        ),
        name="attend",
    )(meta, q, fresh, cache)


def project_kernel(row_total, meta_ref, gain_ref, own_ref, mine_ref, other_ref, *refs):
    blocks = refs[:5]
    out_own_ref, out_oth_ref, out_sq_ref, in_ref, w_ref, x_ref, sems = refs[5:]
    place_at = meta_at(row_total)[3]
    x_at, core = meta_ref[place_at], meta_ref[place_at + 2]
    zh, y_at = meta_ref[place_at + 3], meta_ref[place_at + 4]
    _, tokens, depth = in_ref.shape
    half = tokens // 2
    part = depth // NCORE
    width = own_ref.shape[1]
    shifts = (0, NY - 1, 1, 2)

    def loads(i):
        y = (y_at + shifts[i]) % NY
        feature = zh * NY + y
        near = (y - x_at + NX) % NX
        rows = [
            pl.ds(pl.multiple_of((core ^ far) * part, part), part) for far in range(NCORE)
        ]
        copies = [
            (
                own_ref.at[pl.ds(pl.multiple_of(feature * depth, depth), depth)],
                w_ref.at[i, :, 0:width],
            ),
            (mine_ref.at[near, 0:part], w_ref.at[i, rows[0], width : 2 * width]),
            (other_ref.at[near, 0:part], w_ref.at[i, rows[1], width : 2 * width]),
        ]
        if i < 3:
            copies.append((blocks[i], in_ref.at[i]))
        else:
            copies.append((blocks[3], in_ref.at[i, 0:half]))
            copies.append((blocks[4], in_ref.at[i, half:tokens]))
        return [
            pltpu.make_async_copy(source, target, sems.at[i, n])
            for n, (source, target) in enumerate(copies)
        ]

    for i in range(NY):
        for copy in loads(i):
            copy.start()
    sums = None
    for i, shift in enumerate(shifts):
        gain = gain_ref[pl.ds(zh * NY + (y_at + shift) % NY, 1), :]
        for copy in loads(i):
            copy.wait()
        states = in_ref[i].astype(F32)
        squares = jnp.broadcast_to(jnp.sum(states * states, axis=1, keepdims=True), (tokens, HD))
        x_ref[i] = (states * gain).astype(BF16)
        parts = (jnp.dot(x_ref[i], w_ref[i], preferred_element_type=F32), squares)
        sums = parts if sums is None else tuple(p + q for p, q in zip(sums, parts))
    products, squares = sums
    out_own_ref[...] = products[:, 0:width]
    out_oth_ref[0:tokens, :] = products[:, width : 2 * width].astype(BF16)
    out_sq_ref[...] = squares
    turned = jnp.transpose(squares)
    front = turned[0:PAGE, 0 : 2 * HD]
    back = jnp.concatenate([turned[0:PAGE, 2 * HD : 3 * HD]] * 2, axis=1)
    line = lax.broadcasted_iota(jnp.int32, (PAGE, 2 * HD), 0)
    value = jnp.where(line < 3, front, back)
    term = line % 3
    high = value.astype(BF16).astype(F32)
    rest = value - high
    middle = rest.astype(BF16).astype(F32)
    lowest = rest - middle
    split = jnp.where(term == 0, high, jnp.where(term == 1, middle, lowest))
    out_oth_ref[tokens : tokens + PAGE, :] = jnp.where(line < 6, split, 0.0).astype(BF16)


def project(row_total, meta, gain, own, mine, other, blocks):
    tokens, depth = blocks[0].shape
    width = own.shape[1]
    return pl.pallas_call(
        functools.partial(project_kernel, row_total),
        out_shape=(
            jax.ShapeDtypeStruct((tokens, width), F32),
            jax.ShapeDtypeStruct((tokens + PAGE, width), BF16),
            jax.ShapeDtypeStruct((tokens, HD), F32),
        ),
        in_specs=[SMEM, VMEM, HBM, HBM, HBM] + [HBM] * len(blocks),
        out_specs=(VMEM, VMEM, VMEM),
        scratch_shapes=[
            pltpu.VMEM((NY, tokens, depth), BF16),
            pltpu.VMEM((NY, depth, 2 * width), BF16),
            pltpu.VMEM((NY, tokens, depth), BF16),
            pltpu.SemaphoreType.DMA((NY, 5)),
        ],
        compiler_params=params(56),
        cost_estimate=pl.CostEstimate(
            flops=NY * tokens * depth * width * 4,
            bytes_accessed=12 * 1024 * 1024,
            transcendentals=0,
        ),
        name="project",
    )(meta, gain, own, mine, other, *blocks)


def combine_kernel(
    features, row_total, meta_ref, own_ref, sq_ref, got_ref, turn_ref, out_ref
):
    tokens = own_ref.shape[0]
    total = own_ref[...] + got_ref[0:tokens, :].astype(F32)
    terms = got_ref[tokens : tokens + PAGE, :].astype(F32)
    line = lax.broadcasted_iota(jnp.int32, terms.shape, 0)
    front = jnp.sum(jnp.where(line < 3, terms, 0.0), axis=0, keepdims=True)
    back = jnp.sum(jnp.where(line >= 3, terms, 0.0), axis=0, keepdims=True)[:, 0:HD]
    row = jnp.concatenate([front, back], axis=1)
    squares = sq_ref[...] + jnp.transpose(jnp.broadcast_to(row, (HD, tokens)))
    inv = lax.rsqrt(squares * (1.0 / features) + 1e-05)
    turn = turn_ref[...]
    other = pltpu.roll(turn, HD // 2, 1)
    in_front = lax.broadcasted_iota(jnp.int32, turn.shape, 1) < HD // 2
    cosine = jnp.where(in_front, turn, other)
    sine = jnp.where(in_front, -other, turn)
    keys = total[:, :HD] * inv
    turned = keys * cosine + pltpu.roll(keys, HD // 2, 1) * sine
    page_rows = jnp.concatenate([turned, total[:, HD:] * inv], axis=1)
    len_at, rows_at, target_at, _ = meta_at(row_total)
    token = lax.broadcasted_iota(jnp.int32, (PAGE, page_rows.shape[1]), 0)
    for k in range(MIG):
        length = meta_ref[len_at + meta_ref[rows_at + k]]
        kept = length - (length - 1) // PAGE * PAGE
        page = jnp.where(token < kept, page_rows[k * PAGE : (k + 1) * PAGE], 0.0)
        out_ref[meta_ref[target_at + k] * 2 + k % 2] = page.astype(BF16)


def combine(features, row_total, meta, own, squares, got, turn, members):
    return pl.pallas_call(
        functools.partial(combine_kernel, features, row_total),
        out_shape=jax.ShapeDtypeStruct((members * 2, PAGE, own.shape[1]), BF16),
        in_specs=[SMEM] + [VMEM] * 4,
        out_specs=VMEM,
        compiler_params=params(10),
        name="combine",
    )(meta, own, squares, got, turn)


def assemble_kernel(row_total, meta_ref, counts_ref, *refs):
    kept_refs, other_ref, dirty_ref, out_ref = refs[:NX], refs[NX], refs[NX + 1], refs[NX + 2]
    place_at = meta_at(row_total)[3]
    x_at, z_at, core_at = (meta_ref[place_at + i] for i in range(3))

    for d in range(NX):
        x = (x_at - d + NX) % NX
        near = (x - x_at + NX) % NX
        for far_core in range(NCORE):

            def one(z, carry, d=d, x=x, near=near, far_core=far_core):
                far_z = z ^ z_at
                source = (x * NZL + z) * NCORE + (core_at ^ far_core)
                entry = (far_core * NX + near) * NZL + far_z
                first = counts_ref[2 * entry]
                second = counts_ref[2 * entry + 1]
                for m in range(MAXP):
                    behind = (m >= first).astype(jnp.int32)
                    index = jnp.clip(m - behind, 0, STORED - 1)
                    if far_core == 0:
                        kept = kept_refs[d][z, index]
                    else:
                        kept = other_ref[d, z, index]
                    made = dirty_ref[source * 2 + behind]
                    is_made = (m == first - 1) | (m == first + second - 1)
                    page = jnp.where(is_made, made, kept)
                    out_ref[source * MAXP + m] = jnp.where(
                        m < first + second, page, jnp.zeros_like(page)
                    )
                return carry

            lax.fori_loop(0, NZL, one, 0, unroll=2)


def assemble(row_total, meta, counts, kept, other, dirty, members):
    lanes = dirty.shape[-1]
    return pl.pallas_call(
        functools.partial(assemble_kernel, row_total),
        out_shape=jax.ShapeDtypeStruct((members * MAXP, PAGE, lanes), dirty.dtype),
        in_specs=[SMEM, SMEM] + [VMEM] * (NX + 2),
        out_specs=VMEM,
        compiler_params=params(14),
        name="assemble",
    )(meta, counts, *kept, other, dirty)


def exchange(pages, members, each):
    lanes = pages.shape[-1]
    moved = lax.all_to_all(
        pages.reshape(members, each * PAGE, lanes), "inst", split_axis=0, concat_axis=0, tiled=True
    )
    return moved.reshape(members * each, PAGE, lanes)


def per_device(
    queries,
    new_kv,
    kv_cache,
    block_table,
    lengths,
    mig_rows,
    mig_target,
    dirty_hidden,
    norm_gain,
    kv_weight,
):
    members = lax.axis_size("inst")
    inst = lax.axis_index("inst")
    tp = lax.axis_index("tp")
    x_at, z_lo, core = inst // (NZL * NCORE), inst // NCORE % NZL, inst % NCORE
    zh, y_at = tp // NY, tp % NY
    tokens = MIG * PAGE
    depth = dirty_hidden.shape[-1]
    features = depth * TP
    half_features = depth * NY

    row_count = queries.shape[0]
    meta = meta_of(block_table, lengths, mig_rows, mig_target, (x_at, z_lo, core, zh, y_at))

    hidden = dirty_hidden.reshape(tokens, depth)
    from_below = send(hidden, dy=1)
    from_above = send(hidden, dy=-1)

    picked = mig_rows[:, None] == jnp.arange(row_count, dtype=jnp.int32)[None, :]
    mig_len = jnp.sum(jnp.where(picked, lengths[None, :], 0), axis=1)
    mig_pages = (mig_len + PAGE - 1) // PAGE

    slice_rows = half_features // (NX * NCORE)
    begin = (1 - zh) * half_features + (x_at * NCORE + core) * slice_rows
    width = kv_weight.shape[1]
    notes = jnp.pad(
        jnp.stack([mig_target, mig_pages]).astype(BF16), ((0, PAGE - 2), (0, width - MIG))
    )
    notes = jnp.concatenate([notes[:2], send(notes, zl_xor=1)[:2]], axis=0)
    outgoing_slice = jnp.concatenate(
        [
            lax.dynamic_slice_in_dim(kv_weight, begin, slice_rows, axis=0),
            jnp.pad(notes, ((0, PAGE - 4), (0, 0))),
        ],
        axis=0,
    )
    slice_here = send(outgoing_slice, dzh=1, zl_xor=2)
    noted = jnp.concatenate(
        [slice_here[:slice_rows], notes, slice_here[slice_rows : slice_rows + PAGE - 4]], axis=0
    )
    packed = pack(meta, row_count, kv_cache)
    noted, from_below, from_above, packed = lax.optimization_barrier(
        (noted, from_below, from_above, packed)
    )
    across_top = send(from_below[: tokens // 2], dy=1)
    across_bottom = send(from_above[tokens // 2 :], dy=-1)
    slices = jnp.stack([noted] + [send(noted, dx=-d) for d in range(1, NX)])

    lines = [
        [(x * NZL + z) * NCORE + c for z in range(NZL)] for x in range(NX) for c in range(NCORE)
    ]
    by_z = lax.all_to_all(
        packed, "inst", split_axis=0, concat_axis=0, axis_index_groups=lines, tiled=True
    )

    offsets = jnp.arange(PAGE, dtype=jnp.int32)
    positions = ((mig_pages - 1) * PAGE)[:, None] + offsets[None, :]
    half_dim = HD // 2
    frequency = jnp.exp(
        jnp.arange(half_dim, dtype=F32) * (-2.0 * math.log(500000.0) / HD)
    )
    angles = positions.reshape(tokens).astype(F32)[:, None] * frequency[None, :]
    turn = jnp.concatenate([jnp.cos(angles), jnp.sin(angles)], axis=1)

    gain = norm_gain.astype(F32).reshape(TP, depth)

    slices, across_top, across_bottom = lax.optimization_barrier(
        (slices, across_top, across_bottom)
    )
    other_slices = send(slices, dcore=1)
    own, outgoing, squares = project(
        row_count,
        meta,
        gain,
        kv_weight,
        slices,
        other_slices,
        (hidden, from_below, from_above, across_top, across_bottom),
    )
    outgoing, by_z = lax.optimization_barrier((outgoing, by_z))
    got = send(outgoing, dzh=1)

    by_x = [by_z[:, d] for d in range(NX)]
    by_x = [by_x[0]] + [send(by_x[d], dx=d) for d in range(1, NX)]
    lines = slice(slice_rows, slice_rows + 2 * NZL)
    heard = jnp.stack([slices[:, lines, :MIG], other_slices[:, lines, :MIG]])
    heard = heard.reshape(NCORE, NX, NZL, 2, MIG)
    aimed_here = heard[..., 0, :] == inst.astype(BF16)
    counts = jnp.sum(
        jnp.where(aimed_here, heard[..., 1, :], jnp.zeros((), BF16))
        .astype(F32)
        .reshape(NCORE, NX, NZL, PAIRS, 2),
        axis=3,
    ).astype(jnp.int32)
    got, counts, turn = lax.optimization_barrier((got, counts, turn))
    made = combine(features, row_count, meta, own, squares, got, turn, members)
    dirty = exchange(made, members, 2)

    heads = queries.shape[-1] // HD
    q = queries.reshape(row_count, 2 * heads, HD)
    fresh = jnp.pad(new_kv, ((0, 0), (0, PAGE - 2), (0, 0)))
    q, fresh, _ = lax.optimization_barrier((q, fresh, made))
    decoded = attend(0, row_count, q, fresh, kv_cache, meta)
    decoded = decoded.reshape(row_count, 2, heads * HD)
    other_kept = send(jnp.stack([part[:, STORED:] for part in by_x]), dcore=1)
    dirty, decoded = lax.optimization_barrier((dirty, decoded))
    mig_kv = assemble(
        row_count, meta, counts.reshape(-1), by_x, other_kept, dirty, members
    )
    return decoded, mig_kv


def solution(mesh):
    return jax.shard_map(
        per_device,
        mesh=mesh,
        in_specs=(
            P("inst", None, "tp"),
            P("inst", None, "tp"),
            P("inst", None, "tp"),
            P("inst", None),
            P("inst"),
            P("inst"),
            P("inst"),
            P("inst", None, "tp"),
            P(),
            P(None, "tp"),
        ),
        out_specs=(P("inst", None, "tp"), P("inst", None, "tp")),
        check_vma=False,
    )
```

```python
import functools
import math

import jax
import jax.numpy as jnp
from jax import lax
from jax.experimental import pallas as pl
from jax.experimental.pallas import tpu as pltpu
from jax.sharding import PartitionSpec as P

HD = 128
PAGE = 16
MAXP = 8
MIG = 24
PAIRS = MIG // 2
STORED = MAXP - 2
NX, NZL, NCORE, NZH, NY = 4, 4, 2, 2, 4
TP = NZH * NY
AXES = ("inst", "tp")
F32 = jnp.float32
BF16 = jnp.bfloat16


def index_of(x, zl, core, zh, y):
    return (((x * NZL + zl) * NCORE) + core) * TP + zh * NY + y


def moves(dx=0, dcore=0, dzh=0, dy=0, zl_xor=0):
    pairs = []
    for x in range(NX):
        for zl in range(NZL):
            for core in range(NCORE):
                for zh in range(NZH):
                    for y in range(NY):
                        pairs.append(
                            (
                                index_of(x, zl, core, zh, y),
                                index_of(
                                    (x + dx) % NX,
                                    zl ^ zl_xor,
                                    (core + dcore) % NCORE,
                                    (zh + dzh) % NZH,
                                    (y + dy) % NY,
                                ),
                            )
                        )
    return pairs


def send(value, **by):
    return lax.ppermute(value, AXES, moves(**by))


def params(mebibytes):
    return pltpu.CompilerParams(vmem_limit_bytes=mebibytes * 1024 * 1024)


SMEM = pl.BlockSpec(memory_space=pltpu.SMEM)
VMEM = pl.BlockSpec(memory_space=pltpu.VMEM)
HBM = pl.BlockSpec(memory_space=pltpu.HBM)


def meta_of(table, lengths, rows, target, place):
    parts = [table.reshape(-1), lengths, rows, target, jnp.stack(place)]
    return jnp.concatenate([p.astype(jnp.int32) for p in parts])


def meta_at(row_count):
    lengths = row_count * MAXP
    rows = lengths + row_count
    target = rows + MIG
    return lengths, rows, target, target + MIG


def pack_kernel(row_count, meta_ref, cache_ref, out_ref, held_ref, in_sems, out_sems):
    len_at, rows_at, target_at, place_at = meta_at(row_count)
    x_at, core_at = meta_ref[place_at], meta_ref[place_at + 2]
    for c in range(PAIRS):
        first = meta_ref[rows_at + 2 * c]
        second = meta_ref[rows_at + 2 * c + 1]
        front = (meta_ref[len_at + first] + PAGE - 1) // PAGE - 1
        for m in range(STORED):
            in_front = m < front
            row = jnp.where(in_front, first, second)
            slot = jnp.where(in_front, m, jnp.minimum(m - front, MAXP - 1))
            page = meta_ref[row * MAXP + slot]
            pltpu.make_async_copy(
                cache_ref.at[page], held_ref.at[c, m], in_sems.at[c * STORED + m]
            ).start()

    def out_copy(c):
        target = meta_ref[target_at + 2 * c]
        x, z, core = target // (NZL * NCORE), target // NCORE % NZL, target % NCORE
        far_x = (x - x_at + NX) % NX
        return pltpu.make_async_copy(
            held_ref.at[c],
            out_ref.at[z, far_x, pl.ds((core ^ core_at) * STORED, STORED)],
            out_sems.at[c],
        )

    for c in range(PAIRS):
        for m in range(STORED):
            pltpu.make_async_copy(
                cache_ref.at[0], held_ref.at[c, m], in_sems.at[c * STORED + m]
            ).wait()
        out_copy(c).start()
    for c in range(PAIRS):
        out_copy(c).wait()


def pack(meta, row_count, cache):
    lanes = cache.shape[-1]
    return pl.pallas_call(
        functools.partial(pack_kernel, row_count),
        out_shape=jax.ShapeDtypeStruct(
            (NZL, NX, NCORE * STORED, PAGE, lanes), cache.dtype
        ),
        in_specs=[SMEM, HBM],
        out_specs=HBM,
        scratch_shapes=[
            pltpu.VMEM((PAIRS, STORED, PAGE, lanes), cache.dtype),
            pltpu.SemaphoreType.DMA((PAIRS * STORED,)),
            pltpu.SemaphoreType.DMA((PAIRS,)),
        ],
        compiler_params=params(60),
        cost_estimate=pl.CostEstimate(flops=0, bytes_accessed=4 * 1024 * 1024, transcendentals=0),
        name="pack",
    )(meta, cache)


def attend_kernel(start, row_total, meta_ref, q_ref, new_ref, cache_ref, out_ref):
    row_count, heads, _ = q_ref.shape
    len_at = meta_at(row_total)[0]
    group = 8
    span = MAXP * PAGE + PAGE
    scale = 1.0 / math.sqrt(HD)
    column = lax.broadcasted_iota(jnp.int32, (heads, span), 1)
    step = lax.broadcasted_iota(jnp.int32, (heads, span), 0) // (heads // 2)
    own = (column >= MAXP * PAGE) & (column - MAXP * PAGE <= step)

    def body(i, carry):
        base = i * group
        scores = []
        values = []
        for u in range(group):
            r = base + u
            at = (start + r) * MAXP
            parts = [cache_ref[meta_ref[at + b]] for b in range(MAXP)] + [new_ref[r]]
            tokens = jnp.concatenate(parts, axis=0)
            raw = lax.dot_general(
                q_ref[r], tokens[:, :HD], (((1,), (1,)), ((), ())), preferred_element_type=F32
            )
            seen = (column < meta_ref[len_at + start + r]) | own
            scores.append(jnp.where(seen, raw * scale, -jnp.inf))
            values.append(tokens[:, HD:])
        stacked = jnp.concatenate(scores, axis=0)
        raised = jnp.exp(stacked - jnp.max(stacked, axis=-1, keepdims=True))
        weights = (raised / jnp.sum(raised, axis=-1, keepdims=True)).astype(BF16)
        mixed = [
            jnp.dot(weights[u * heads : (u + 1) * heads], values[u], preferred_element_type=F32)
            for u in range(group)
        ]
        for u in range(group):
            out_ref[base + u] = mixed[u].astype(BF16)
        return carry

    lax.fori_loop(0, row_count // group, body, 0)


def attend(start, row_total, q, fresh, cache, meta):
    row_count, heads, _ = q.shape
    return pl.pallas_call(
        functools.partial(attend_kernel, start, row_total),
        out_shape=jax.ShapeDtypeStruct((row_count, heads, HD), BF16),
        in_specs=[SMEM, VMEM, VMEM, VMEM],
        out_specs=VMEM,
        compiler_params=params(14),
        cost_estimate=pl.CostEstimate(
            flops=row_count * 16 * 144 * 128 * 4,
            bytes_accessed=row_count * 512 * 1024,
            transcendentals=0,
        ),
        name="attend",
    )(meta, q, fresh, cache)


def project_kernel(row_total, meta_ref, gain_ref, own_ref, mine_ref, other_ref, *refs):
    blocks = refs[:5]
    out_own_ref, out_oth_ref, out_sq_ref, in_ref, w_ref, x_ref, sems = refs[5:]
    place_at = meta_at(row_total)[3]
    x_at, core = meta_ref[place_at], meta_ref[place_at + 2]
    zh, y_at = meta_ref[place_at + 3], meta_ref[place_at + 4]
    _, tokens, depth = in_ref.shape
    half = tokens // 2
    part = depth // NCORE
    width = own_ref.shape[1]
    shifts = (0, NY - 1, 1, 2)

    def loads(i):
        y = (y_at + shifts[i]) % NY
        feature = zh * NY + y
        near = (y - x_at + NX) % NX
        rows = [
            pl.ds(pl.multiple_of((core ^ far) * part, part), part) for far in range(NCORE)
        ]
        copies = [
            (
                own_ref.at[pl.ds(pl.multiple_of(feature * depth, depth), depth)],
                w_ref.at[i, :, 0:width],
            ),
            (mine_ref.at[near, 0:part], w_ref.at[i, rows[0], width : 2 * width]),
            (other_ref.at[near, 0:part], w_ref.at[i, rows[1], width : 2 * width]),
        ]
        if i < 3:
            copies.append((blocks[i], in_ref.at[i]))
        else:
            copies.append((blocks[3], in_ref.at[i, 0:half]))
            copies.append((blocks[4], in_ref.at[i, half:tokens]))
        return [
            pltpu.make_async_copy(source, target, sems.at[i, n])
            for n, (source, target) in enumerate(copies)
        ]

    for i in range(NY):
        for copy in loads(i):
            copy.start()
    sums = None
    for i, shift in enumerate(shifts):
        gain = gain_ref[pl.ds(zh * NY + (y_at + shift) % NY, 1), :]
        for copy in loads(i):
            copy.wait()
        states = in_ref[i].astype(F32)
        squares = jnp.broadcast_to(jnp.sum(states * states, axis=1, keepdims=True), (tokens, HD))
        x_ref[i] = (states * gain).astype(BF16)
        parts = (jnp.dot(x_ref[i], w_ref[i], preferred_element_type=F32), squares)
        sums = parts if sums is None else tuple(p + q for p, q in zip(sums, parts))
    products, squares = sums
    out_own_ref[...] = products[:, 0:width]
    out_oth_ref[0:tokens, :] = products[:, width : 2 * width].astype(BF16)
    out_sq_ref[...] = squares
    turned = jnp.transpose(squares)
    front = turned[0:PAGE, 0 : 2 * HD]
    back = jnp.concatenate([turned[0:PAGE, 2 * HD : 3 * HD]] * 2, axis=1)
    line = lax.broadcasted_iota(jnp.int32, (PAGE, 2 * HD), 0)
    value = jnp.where(line < 3, front, back)
    term = line % 3
    high = value.astype(BF16).astype(F32)
    rest = value - high
    middle = rest.astype(BF16).astype(F32)
    lowest = rest - middle
    split = jnp.where(term == 0, high, jnp.where(term == 1, middle, lowest))
    out_oth_ref[tokens : tokens + PAGE, :] = jnp.where(line < 6, split, 0.0).astype(BF16)


def project(row_total, meta, gain, own, mine, other, blocks):
    tokens, depth = blocks[0].shape
    width = own.shape[1]
    return pl.pallas_call(
        functools.partial(project_kernel, row_total),
        out_shape=(
            jax.ShapeDtypeStruct((tokens, width), F32),
            jax.ShapeDtypeStruct((tokens + PAGE, width), BF16),
            jax.ShapeDtypeStruct((tokens, HD), F32),
        ),
        in_specs=[SMEM, VMEM, HBM, HBM, HBM] + [HBM] * len(blocks),
        out_specs=(VMEM, VMEM, VMEM),
        scratch_shapes=[
            pltpu.VMEM((NY, tokens, depth), BF16),
            pltpu.VMEM((NY, depth, 2 * width), BF16),
            pltpu.VMEM((NY, tokens, depth), BF16),
            pltpu.SemaphoreType.DMA((NY, 5)),
        ],
        compiler_params=params(56),
        cost_estimate=pl.CostEstimate(
            flops=NY * tokens * depth * width * 4,
            bytes_accessed=12 * 1024 * 1024,
            transcendentals=0,
        ),
        name="project",
    )(meta, gain, own, mine, other, *blocks)


def combine_kernel(
    features, row_total, meta_ref, own_ref, sq_ref, got_ref, turn_ref, out_ref
):
    tokens = own_ref.shape[0]
    total = own_ref[...] + got_ref[0:tokens, :].astype(F32)
    terms = got_ref[tokens : tokens + PAGE, :].astype(F32)
    line = lax.broadcasted_iota(jnp.int32, terms.shape, 0)
    front = jnp.sum(jnp.where(line < 3, terms, 0.0), axis=0, keepdims=True)
    back = jnp.sum(jnp.where(line >= 3, terms, 0.0), axis=0, keepdims=True)[:, 0:HD]
    row = jnp.concatenate([front, back], axis=1)
    squares = sq_ref[...] + jnp.transpose(jnp.broadcast_to(row, (HD, tokens)))
    inv = lax.rsqrt(squares * (1.0 / features) + 1e-05)
    turn = turn_ref[...]
    other = pltpu.roll(turn, HD // 2, 1)
    in_front = lax.broadcasted_iota(jnp.int32, turn.shape, 1) < HD // 2
    cosine = jnp.where(in_front, turn, other)
    sine = jnp.where(in_front, -other, turn)
    keys = total[:, :HD] * inv
    turned = keys * cosine + pltpu.roll(keys, HD // 2, 1) * sine
    page_rows = jnp.concatenate([turned, total[:, HD:] * inv], axis=1)
    len_at, rows_at, target_at, _ = meta_at(row_total)
    token = lax.broadcasted_iota(jnp.int32, (PAGE, page_rows.shape[1]), 0)
    for k in range(MIG):
        length = meta_ref[len_at + meta_ref[rows_at + k]]
        kept = length - (length - 1) // PAGE * PAGE
        page = jnp.where(token < kept, page_rows[k * PAGE : (k + 1) * PAGE], 0.0)
        out_ref[meta_ref[target_at + k] * 2 + k % 2] = page.astype(BF16)


def combine(features, row_total, meta, own, squares, got, turn, members):
    return pl.pallas_call(
        functools.partial(combine_kernel, features, row_total),
        out_shape=jax.ShapeDtypeStruct((members * 2, PAGE, own.shape[1]), BF16),
        in_specs=[SMEM] + [VMEM] * 4,
        out_specs=VMEM,
        compiler_params=params(10),
        name="combine",
    )(meta, own, squares, got, turn)


def assemble_kernel(row_total, meta_ref, counts_ref, *refs):
    kept_refs, other_ref, dirty_ref, out_ref = refs[:NX], refs[NX], refs[NX + 1], refs[NX + 2]
    place_at = meta_at(row_total)[3]
    x_at, z_at, core_at = (meta_ref[place_at + i] for i in range(3))

    for d in range(NX):
        x = (x_at - d + NX) % NX
        near = (x - x_at + NX) % NX
        for far_core in range(NCORE):

            def one(z, carry, d=d, x=x, near=near, far_core=far_core):
                far_z = z ^ z_at
                source = (x * NZL + z) * NCORE + (core_at ^ far_core)
                entry = (far_z * NCORE + far_core) * NX + near
                first = counts_ref[2 * entry]
                second = counts_ref[2 * entry + 1]
                for m in range(MAXP):
                    behind = (m >= first).astype(jnp.int32)
                    index = jnp.clip(m - behind, 0, STORED - 1)
                    if far_core == 0:
                        kept = kept_refs[d][z, index]
                    else:
                        kept = other_ref[d, z, index]
                    made = dirty_ref[source * 2 + behind]
                    is_made = (m == first - 1) | (m == first + second - 1)
                    page = jnp.where(is_made, made, kept)
                    out_ref[source * MAXP + m] = jnp.where(
                        m < first + second, page, jnp.zeros_like(page)
                    )
                return carry

            lax.fori_loop(0, NZL, one, 0, unroll=2)


def assemble(row_total, meta, counts, kept, other, dirty, members):
    lanes = dirty.shape[-1]
    return pl.pallas_call(
        functools.partial(assemble_kernel, row_total),
        out_shape=jax.ShapeDtypeStruct((members * MAXP, PAGE, lanes), dirty.dtype),
        in_specs=[SMEM, SMEM] + [VMEM] * (NX + 2),
        out_specs=VMEM,
        compiler_params=params(14),
        name="assemble",
    )(meta, counts, *kept, other, dirty)


def exchange(pages, members, each):
    lanes = pages.shape[-1]
    moved = lax.all_to_all(
        pages.reshape(members, each * PAGE, lanes), "inst", split_axis=0, concat_axis=0, tiled=True
    )
    return moved.reshape(members * each, PAGE, lanes)


def per_device(
    queries,
    new_kv,
    kv_cache,
    block_table,
    lengths,
    mig_rows,
    mig_target,
    dirty_hidden,
    norm_gain,
    kv_weight,
):
    members = lax.axis_size("inst")
    inst = lax.axis_index("inst")
    tp = lax.axis_index("tp")
    x_at, z_lo, core = inst // (NZL * NCORE), inst // NCORE % NZL, inst % NCORE
    zh, y_at = tp // NY, tp % NY
    tokens = MIG * PAGE
    depth = dirty_hidden.shape[-1]
    features = depth * TP
    half_features = depth * NY

    row_count = queries.shape[0]
    meta = meta_of(block_table, lengths, mig_rows, mig_target, (x_at, z_lo, core, zh, y_at))

    hidden = dirty_hidden.reshape(tokens, depth)
    from_below = send(hidden, dy=1)
    from_above = send(hidden, dy=-1)

    picked = mig_rows[:, None] == jnp.arange(row_count, dtype=jnp.int32)[None, :]
    mig_len = jnp.sum(jnp.where(picked, lengths[None, :], 0), axis=1)
    mig_pages = (mig_len + PAGE - 1) // PAGE

    slice_rows = half_features // (NX * NCORE)
    begin = (1 - zh) * half_features + (x_at * NCORE + core) * slice_rows
    width = kv_weight.shape[1]
    slice_here = send(
        lax.dynamic_slice_in_dim(kv_weight, begin, slice_rows, axis=0), dzh=1, zl_xor=2
    )
    notes = jnp.pad(
        jnp.stack([mig_target, mig_pages]).astype(BF16), ((0, PAGE - 2), (0, width - MIG))
    )
    packed = pack(meta, row_count, kv_cache)
    slice_here, from_below, from_above, _ = lax.optimization_barrier(
        (slice_here, from_below, from_above, packed)
    )
    noted = jnp.concatenate([slice_here, notes], axis=0)
    across_top = send(from_below[: tokens // 2], dy=1)
    across_bottom = send(from_above[tokens // 2 :], dy=-1)
    slices = jnp.stack([noted] + [send(noted, dx=-d) for d in range(1, NX)])

    lines = [
        [(x * NZL + z) * NCORE + c for z in range(NZL)] for x in range(NX) for c in range(NCORE)
    ]
    by_z = lax.all_to_all(
        packed, "inst", split_axis=0, concat_axis=0, axis_index_groups=lines, tiled=True
    )

    offsets = jnp.arange(PAGE, dtype=jnp.int32)
    positions = ((mig_pages - 1) * PAGE)[:, None] + offsets[None, :]
    half_dim = HD // 2
    frequency = jnp.exp(
        jnp.arange(half_dim, dtype=F32) * (-2.0 * math.log(500000.0) / HD)
    )
    angles = positions.reshape(tokens).astype(F32)[:, None] * frequency[None, :]
    turn = jnp.concatenate([jnp.cos(angles), jnp.sin(angles)], axis=1)

    gain = norm_gain.astype(F32).reshape(TP, depth)

    slices, across_top, across_bottom = lax.optimization_barrier(
        (slices, across_top, across_bottom)
    )
    other_slices = send(slices, dcore=1)
    own, outgoing, squares = project(
        row_count,
        meta,
        gain,
        kv_weight,
        slices,
        other_slices,
        (hidden, from_below, from_above, across_top, across_bottom),
    )
    outgoing, by_z = lax.optimization_barrier((outgoing, by_z))
    got = send(outgoing, dzh=1)

    by_x = [by_z[:, d] for d in range(NX)]
    by_x = [by_x[0]] + [send(by_x[d], dx=d) for d in range(1, NX)]
    heads = queries.shape[-1] // HD
    q = queries.reshape(row_count, 2 * heads, HD)
    fresh = jnp.pad(new_kv, ((0, 0), (0, PAGE - 2), (0, 0)))
    q, fresh, _ = lax.optimization_barrier((q, fresh, outgoing))
    decoded = attend(0, row_count, q, fresh, kv_cache, meta)
    decoded = decoded.reshape(row_count, 2, heads * HD)
    got, turn, decoded = lax.optimization_barrier((got, turn, decoded))
    made = combine(features, row_count, meta, own, squares, got, turn, members)

    lines = slice(slice_rows, slice_rows + 2)
    heard = jnp.stack([slices[:, lines, :MIG], other_slices[:, lines, :MIG]])
    heard, _ = lax.optimization_barrier((heard, made))
    heard = jnp.stack([heard, send(heard, zl_xor=1)])
    heard = jnp.concatenate([heard, send(heard, zl_xor=2)])
    aimed_here = heard[..., 0, :] == inst.astype(BF16)
    counts = jnp.sum(
        jnp.where(aimed_here, heard[..., 1, :], jnp.zeros((), BF16))
        .astype(F32)
        .reshape(NZL, NCORE, NX, PAIRS, 2),
        axis=3,
    ).astype(jnp.int32)
    dirty = exchange(made, members, 2)

    other_kept = send(jnp.stack([part[:, STORED:] for part in by_x]), dcore=1)
    mig_kv = assemble(
        row_count, meta, counts.reshape(-1), by_x, other_kept, dirty, members
    )
    return decoded, mig_kv


def solution(mesh):
    return jax.shard_map(
        per_device,
        mesh=mesh,
        in_specs=(
            P("inst", None, "tp"),
            P("inst", None, "tp"),
            P("inst", None, "tp"),
            P("inst", None),
            P("inst"),
            P("inst"),
            P("inst"),
            P("inst", None, "tp"),
            P(),
            P(None, "tp"),
        ),
        out_specs=(P("inst", None, "tp"), P("inst", None, "tp")),
        check_vma=False,
    )
```

```python
import functools
import math

import jax
import jax.numpy as jnp
from jax import lax
from jax.experimental import pallas as pl
from jax.experimental.pallas import tpu as pltpu
from jax.sharding import PartitionSpec as P

HD = 128
PAGE = 16
MAXP = 8
MIG = 24
PAIRS = MIG // 2
STORED = MAXP - 2
NX, NZL, NCORE, NZH, NY = 4, 4, 2, 2, 4
TP = NZH * NY
AXES = ("inst", "tp")
F32 = jnp.float32
BF16 = jnp.bfloat16


def index_of(x, zl, core, zh, y):
    return (((x * NZL + zl) * NCORE) + core) * TP + zh * NY + y


def moves(dx=0, dcore=0, dzh=0, dy=0, zl_xor=0):
    pairs = []
    for x in range(NX):
        for zl in range(NZL):
            for core in range(NCORE):
                for zh in range(NZH):
                    for y in range(NY):
                        pairs.append(
                            (
                                index_of(x, zl, core, zh, y),
                                index_of(
                                    (x + dx) % NX,
                                    zl ^ zl_xor,
                                    (core + dcore) % NCORE,
                                    (zh + dzh) % NZH,
                                    (y + dy) % NY,
                                ),
                            )
                        )
    return pairs


def send(value, **by):
    return lax.ppermute(value, AXES, moves(**by))


def params(mebibytes):
    return pltpu.CompilerParams(vmem_limit_bytes=mebibytes * 1024 * 1024)


SMEM = pl.BlockSpec(memory_space=pltpu.SMEM)
VMEM = pl.BlockSpec(memory_space=pltpu.VMEM)
HBM = pl.BlockSpec(memory_space=pltpu.HBM)


def meta_of(table, lengths, rows, target, place):
    parts = [table.reshape(-1), lengths, rows, target, jnp.stack(place)]
    return jnp.concatenate([p.astype(jnp.int32) for p in parts])


def meta_at(row_count):
    lengths = row_count * MAXP
    rows = lengths + row_count
    target = rows + MIG
    return lengths, rows, target, target + MIG


def pack_kernel(row_count, meta_ref, cache_ref, out_ref, held_ref, in_sems, out_sems):
    len_at, rows_at, target_at, place_at = meta_at(row_count)
    x_at, core_at = meta_ref[place_at], meta_ref[place_at + 2]
    for c in range(PAIRS):
        first = meta_ref[rows_at + 2 * c]
        second = meta_ref[rows_at + 2 * c + 1]
        front = (meta_ref[len_at + first] + PAGE - 1) // PAGE - 1
        for m in range(STORED):
            in_front = m < front
            row = jnp.where(in_front, first, second)
            slot = jnp.where(in_front, m, jnp.minimum(m - front, MAXP - 1))
            page = meta_ref[row * MAXP + slot]
            pltpu.make_async_copy(
                cache_ref.at[page], held_ref.at[c, m], in_sems.at[c * STORED + m]
            ).start()

    def out_copy(c):
        target = meta_ref[target_at + 2 * c]
        x, z, core = target // (NZL * NCORE), target // NCORE % NZL, target % NCORE
        far_x = (x - x_at + NX) % NX
        return pltpu.make_async_copy(
            held_ref.at[c],
            out_ref.at[z, far_x, pl.ds((core ^ core_at) * STORED, STORED)],
            out_sems.at[c],
        )

    for c in range(PAIRS):
        for m in range(STORED):
            pltpu.make_async_copy(
                cache_ref.at[0], held_ref.at[c, m], in_sems.at[c * STORED + m]
            ).wait()
        out_copy(c).start()
    for c in range(PAIRS):
        out_copy(c).wait()


def pack(meta, row_count, cache):
    lanes = cache.shape[-1]
    return pl.pallas_call(
        functools.partial(pack_kernel, row_count),
        out_shape=jax.ShapeDtypeStruct(
            (NZL, NX, NCORE * STORED, PAGE, lanes), cache.dtype
        ),
        in_specs=[SMEM, HBM],
        out_specs=HBM,
        scratch_shapes=[
            pltpu.VMEM((PAIRS, STORED, PAGE, lanes), cache.dtype),
            pltpu.SemaphoreType.DMA((PAIRS * STORED,)),
            pltpu.SemaphoreType.DMA((PAIRS,)),
        ],
        compiler_params=params(60),
        cost_estimate=pl.CostEstimate(flops=0, bytes_accessed=4 * 1024 * 1024, transcendentals=0),
        name="pack",
    )(meta, cache)


def attend_kernel(start, row_total, meta_ref, q_ref, new_ref, cache_ref, out_ref):
    row_count, heads, _ = q_ref.shape
    len_at = meta_at(row_total)[0]
    group = 8
    span = MAXP * PAGE + PAGE
    scale = 1.0 / math.sqrt(HD)
    column = lax.broadcasted_iota(jnp.int32, (heads, span), 1)
    step = lax.broadcasted_iota(jnp.int32, (heads, span), 0) // (heads // 2)
    own = (column >= MAXP * PAGE) & (column - MAXP * PAGE <= step)

    def body(i, carry):
        base = i * group
        scores = []
        values = []
        for u in range(group):
            r = base + u
            at = (start + r) * MAXP
            parts = [cache_ref[meta_ref[at + b]] for b in range(MAXP)] + [new_ref[r]]
            tokens = jnp.concatenate(parts, axis=0)
            raw = lax.dot_general(
                q_ref[r], tokens[:, :HD], (((1,), (1,)), ((), ())), preferred_element_type=F32
            )
            seen = (column < meta_ref[len_at + start + r]) | own
            scores.append(jnp.where(seen, raw * scale, -jnp.inf))
            values.append(tokens[:, HD:])
        stacked = jnp.concatenate(scores, axis=0)
        raised = jnp.exp(stacked - jnp.max(stacked, axis=-1, keepdims=True))
        weights = (raised / jnp.sum(raised, axis=-1, keepdims=True)).astype(BF16)
        mixed = [
            jnp.dot(weights[u * heads : (u + 1) * heads], values[u], preferred_element_type=F32)
            for u in range(group)
        ]
        for u in range(group):
            out_ref[base + u] = mixed[u].astype(BF16)
        return carry

    lax.fori_loop(0, row_count // group, body, 0)


def attend(start, row_total, q, fresh, cache, meta):
    row_count, heads, _ = q.shape
    return pl.pallas_call(
        functools.partial(attend_kernel, start, row_total),
        out_shape=jax.ShapeDtypeStruct((row_count, heads, HD), BF16),
        in_specs=[SMEM, VMEM, VMEM, VMEM],
        out_specs=VMEM,
        compiler_params=params(14),
        cost_estimate=pl.CostEstimate(
            flops=row_count * 16 * 144 * 128 * 4,
            bytes_accessed=row_count * 512 * 1024,
            transcendentals=0,
        ),
        name="attend",
    )(meta, q, fresh, cache)


def project_kernel(row_total, meta_ref, gain_ref, own_ref, mine_ref, other_ref, *refs):
    blocks = refs[:5]
    out_own_ref, out_oth_ref, out_sq_ref, in_ref, w_ref, x_ref, sems = refs[5:]
    place_at = meta_at(row_total)[3]
    x_at, core = meta_ref[place_at], meta_ref[place_at + 2]
    zh, y_at = meta_ref[place_at + 3], meta_ref[place_at + 4]
    _, tokens, depth = in_ref.shape
    half = tokens // 2
    part = depth // NCORE
    width = own_ref.shape[1]
    shifts = (0, NY - 1, 1, 2)

    def loads(i):
        y = (y_at + shifts[i]) % NY
        feature = zh * NY + y
        near = (y - x_at + NX) % NX
        rows = [
            pl.ds(pl.multiple_of((core ^ far) * part, part), part) for far in range(NCORE)
        ]
        copies = [
            (
                own_ref.at[pl.ds(pl.multiple_of(feature * depth, depth), depth)],
                w_ref.at[i, :, 0:width],
            ),
            (mine_ref.at[near, 0:part], w_ref.at[i, rows[0], width : 2 * width]),
            (other_ref.at[near, 0:part], w_ref.at[i, rows[1], width : 2 * width]),
        ]
        if i < 3:
            copies.append((blocks[i], in_ref.at[i]))
        else:
            copies.append((blocks[3], in_ref.at[i, 0:half]))
            copies.append((blocks[4], in_ref.at[i, half:tokens]))
        return [
            pltpu.make_async_copy(source, target, sems.at[i, n])
            for n, (source, target) in enumerate(copies)
        ]

    for i in range(NY):
        for copy in loads(i):
            copy.start()
    sums = None
    for i, shift in enumerate(shifts):
        gain = gain_ref[pl.ds(zh * NY + (y_at + shift) % NY, 1), :]
        for copy in loads(i):
            copy.wait()
        states = in_ref[i].astype(F32)
        squares = jnp.broadcast_to(jnp.sum(states * states, axis=1, keepdims=True), (tokens, HD))
        x_ref[i] = (states * gain).astype(BF16)
        parts = (jnp.dot(x_ref[i], w_ref[i], preferred_element_type=F32), squares)
        sums = parts if sums is None else tuple(p + q for p, q in zip(sums, parts))
    products, squares = sums
    out_own_ref[...] = products[:, 0:width]
    out_oth_ref[0:tokens, :] = products[:, width : 2 * width].astype(BF16)
    out_sq_ref[...] = squares
    turned = jnp.transpose(squares)
    front = turned[0:PAGE, 0 : 2 * HD]
    back = jnp.concatenate([turned[0:PAGE, 2 * HD : 3 * HD]] * 2, axis=1)
    line = lax.broadcasted_iota(jnp.int32, (PAGE, 2 * HD), 0)
    value = jnp.where(line < 3, front, back)
    term = line % 3
    high = value.astype(BF16).astype(F32)
    rest = value - high
    middle = rest.astype(BF16).astype(F32)
    lowest = rest - middle
    split = jnp.where(term == 0, high, jnp.where(term == 1, middle, lowest))
    out_oth_ref[tokens : tokens + PAGE, :] = jnp.where(line < 6, split, 0.0).astype(BF16)


def project(row_total, meta, gain, own, mine, other, blocks):
    tokens, depth = blocks[0].shape
    width = own.shape[1]
    return pl.pallas_call(
        functools.partial(project_kernel, row_total),
        out_shape=(
            jax.ShapeDtypeStruct((tokens, width), F32),
            jax.ShapeDtypeStruct((tokens + PAGE, width), BF16),
            jax.ShapeDtypeStruct((tokens, HD), F32),
        ),
        in_specs=[SMEM, VMEM, HBM, HBM, HBM] + [HBM] * len(blocks),
        out_specs=(VMEM, VMEM, VMEM),
        scratch_shapes=[
            pltpu.VMEM((NY, tokens, depth), BF16),
            pltpu.VMEM((NY, depth, 2 * width), BF16),
            pltpu.VMEM((NY, tokens, depth), BF16),
            pltpu.SemaphoreType.DMA((NY, 5)),
        ],
        compiler_params=params(56),
        cost_estimate=pl.CostEstimate(
            flops=NY * tokens * depth * width * 4,
            bytes_accessed=12 * 1024 * 1024,
            transcendentals=0,
        ),
        name="project",
    )(meta, gain, own, mine, other, *blocks)


def combine_kernel(
    features, row_total, meta_ref, own_ref, sq_ref, got_ref, turn_ref, out_ref
):
    tokens = own_ref.shape[0]
    total = own_ref[...] + got_ref[0:tokens, :].astype(F32)
    terms = got_ref[tokens : tokens + PAGE, :].astype(F32)
    line = lax.broadcasted_iota(jnp.int32, terms.shape, 0)
    front = jnp.sum(jnp.where(line < 3, terms, 0.0), axis=0, keepdims=True)
    back = jnp.sum(jnp.where(line >= 3, terms, 0.0), axis=0, keepdims=True)[:, 0:HD]
    row = jnp.concatenate([front, back], axis=1)
    squares = sq_ref[...] + jnp.transpose(jnp.broadcast_to(row, (HD, tokens)))
    inv = lax.rsqrt(squares * (1.0 / features) + 1e-05)
    turn = turn_ref[...]
    other = pltpu.roll(turn, HD // 2, 1)
    in_front = lax.broadcasted_iota(jnp.int32, turn.shape, 1) < HD // 2
    cosine = jnp.where(in_front, turn, other)
    sine = jnp.where(in_front, -other, turn)
    keys = total[:, :HD] * inv
    turned = keys * cosine + pltpu.roll(keys, HD // 2, 1) * sine
    page_rows = jnp.concatenate([turned, total[:, HD:] * inv], axis=1)
    len_at, rows_at, target_at, _ = meta_at(row_total)
    token = lax.broadcasted_iota(jnp.int32, (PAGE, page_rows.shape[1]), 0)
    for k in range(MIG):
        length = meta_ref[len_at + meta_ref[rows_at + k]]
        kept = length - (length - 1) // PAGE * PAGE
        page = jnp.where(token < kept, page_rows[k * PAGE : (k + 1) * PAGE], 0.0)
        out_ref[meta_ref[target_at + k] * 2 + k % 2] = page.astype(BF16)


def combine(features, row_total, meta, own, squares, got, turn, members):
    return pl.pallas_call(
        functools.partial(combine_kernel, features, row_total),
        out_shape=jax.ShapeDtypeStruct((members * 2, PAGE, own.shape[1]), BF16),
        in_specs=[SMEM] + [VMEM] * 4,
        out_specs=VMEM,
        compiler_params=params(10),
        name="combine",
    )(meta, own, squares, got, turn)


def assemble_kernel(row_total, meta_ref, counts_ref, *refs):
    kept_refs, other_ref, dirty_ref, target_ref, out_ref, sems = refs[:NX], *refs[NX:]
    place_at = meta_at(row_total)[3]
    x_at, z_at, core_at = (meta_ref[place_at + i] for i in range(3))

    chunk = NZL * NCORE * MAXP

    def leave(d):
        x = (x_at - d + NX) % NX
        pages = pl.ds(x * chunk, chunk)
        return pltpu.make_async_copy(out_ref.at[pages], target_ref.at[pages], sems.at[d])

    for d in range(NX):
        x = (x_at - d + NX) % NX
        near = (x - x_at + NX) % NX
        for far_core in range(NCORE):

            def one(z, carry, d=d, x=x, near=near, far_core=far_core):
                far_z = z ^ z_at
                source = (x * NZL + z) * NCORE + (core_at ^ far_core)
                entry = (far_z * NCORE + far_core) * NX + near
                first = counts_ref[2 * entry]
                second = counts_ref[2 * entry + 1]
                for m in range(MAXP):
                    behind = (m >= first).astype(jnp.int32)
                    index = jnp.clip(m - behind, 0, STORED - 1)
                    if far_core == 0:
                        kept = kept_refs[d][z, index]
                    else:
                        kept = other_ref[d, z, index]
                    made = dirty_ref[source * 2 + behind]
                    is_made = (m == first - 1) | (m == first + second - 1)
                    page = jnp.where(is_made, made, kept)
                    out_ref[source * MAXP + m] = jnp.where(
                        m < first + second, page, jnp.zeros_like(page)
                    )
                return carry

            lax.fori_loop(0, NZL, one, 0, unroll=2)
        leave(d).start()
    for d in range(NX):
        leave(d).wait()


def assemble(row_total, meta, counts, kept, other, dirty, members):
    lanes = dirty.shape[-1]
    return pl.pallas_call(
        functools.partial(assemble_kernel, row_total),
        out_shape=jax.ShapeDtypeStruct((members * MAXP, PAGE, lanes), dirty.dtype),
        in_specs=[SMEM, SMEM] + [VMEM] * (NX + 2),
        out_specs=HBM,
        scratch_shapes=[
            pltpu.VMEM((members * MAXP, PAGE, lanes), dirty.dtype),
            pltpu.SemaphoreType.DMA((NX,)),
        ],
        compiler_params=params(14),
        name="assemble",
    )(meta, counts, *kept, other, dirty)


def exchange(pages, members, each):
    lanes = pages.shape[-1]
    moved = lax.all_to_all(
        pages.reshape(members, each * PAGE, lanes), "inst", split_axis=0, concat_axis=0, tiled=True
    )
    return moved.reshape(members * each, PAGE, lanes)


def per_device(
    queries,
    new_kv,
    kv_cache,
    block_table,
    lengths,
    mig_rows,
    mig_target,
    dirty_hidden,
    norm_gain,
    kv_weight,
):
    members = lax.axis_size("inst")
    inst = lax.axis_index("inst")
    tp = lax.axis_index("tp")
    x_at, z_lo, core = inst // (NZL * NCORE), inst // NCORE % NZL, inst % NCORE
    zh, y_at = tp // NY, tp % NY
    tokens = MIG * PAGE
    depth = dirty_hidden.shape[-1]
    features = depth * TP
    half_features = depth * NY

    row_count = queries.shape[0]
    meta = meta_of(block_table, lengths, mig_rows, mig_target, (x_at, z_lo, core, zh, y_at))

    hidden = dirty_hidden.reshape(tokens, depth)
    from_below = send(hidden, dy=1)
    from_above = send(hidden, dy=-1)

    picked = mig_rows[:, None] == jnp.arange(row_count, dtype=jnp.int32)[None, :]
    mig_len = jnp.sum(jnp.where(picked, lengths[None, :], 0), axis=1)
    mig_pages = (mig_len + PAGE - 1) // PAGE

    slice_rows = half_features // (NX * NCORE)
    begin = (1 - zh) * half_features + (x_at * NCORE + core) * slice_rows
    width = kv_weight.shape[1]
    slice_here = send(
        lax.dynamic_slice_in_dim(kv_weight, begin, slice_rows, axis=0), dzh=1, zl_xor=2
    )
    notes = jnp.pad(
        jnp.stack([mig_target, mig_pages]).astype(BF16), ((0, PAGE - 2), (0, width - MIG))
    )
    packed = pack(meta, row_count, kv_cache)
    slice_here, from_below, from_above, _ = lax.optimization_barrier(
        (slice_here, from_below, from_above, packed)
    )
    noted = jnp.concatenate([slice_here, notes], axis=0)
    across_top = send(from_below[: tokens // 2], dy=1)
    across_bottom = send(from_above[tokens // 2 :], dy=-1)
    slices = jnp.stack([noted] + [send(noted, dx=-d) for d in range(1, NX)])

    lines = [
        [(x * NZL + z) * NCORE + c for z in range(NZL)] for x in range(NX) for c in range(NCORE)
    ]
    by_z = lax.all_to_all(
        packed, "inst", split_axis=0, concat_axis=0, axis_index_groups=lines, tiled=True
    )

    offsets = jnp.arange(PAGE, dtype=jnp.int32)
    positions = ((mig_pages - 1) * PAGE)[:, None] + offsets[None, :]
    half_dim = HD // 2
    frequency = jnp.exp(
        jnp.arange(half_dim, dtype=F32) * (-2.0 * math.log(500000.0) / HD)
    )
    angles = positions.reshape(tokens).astype(F32)[:, None] * frequency[None, :]
    turn = jnp.concatenate([jnp.cos(angles), jnp.sin(angles)], axis=1)

    gain = norm_gain.astype(F32).reshape(TP, depth)

    slices, across_top, across_bottom = lax.optimization_barrier(
        (slices, across_top, across_bottom)
    )
    other_slices = send(slices, dcore=1)
    own, outgoing, squares = project(
        row_count,
        meta,
        gain,
        kv_weight,
        slices,
        other_slices,
        (hidden, from_below, from_above, across_top, across_bottom),
    )
    got = send(outgoing, dzh=1)

    heads = queries.shape[-1] // HD
    q = queries.reshape(row_count, 2 * heads, HD)
    fresh = jnp.pad(new_kv, ((0, 0), (0, PAGE - 2), (0, 0)))
    q, fresh, _ = lax.optimization_barrier((q, fresh, outgoing))
    decoded = attend(0, row_count, q, fresh, kv_cache, meta)
    decoded = decoded.reshape(row_count, 2, heads * HD)
    by_z, decoded = lax.optimization_barrier((by_z, decoded))
    lines = slice(slice_rows, slice_rows + 2)
    heard = jnp.stack([slices[:, lines, :MIG], other_slices[:, lines, :MIG]])
    heard, _ = lax.optimization_barrier((heard, outgoing))
    heard_next = send(heard, zl_xor=1)
    by_x = [by_z[:, d] for d in range(NX)]
    got, *by_x = lax.optimization_barrier((got, *by_x))
    by_x = [by_x[0]] + [send(by_x[d], dx=d) for d in range(1, NX)]
    got, turn, heard_next = lax.optimization_barrier((got, turn, heard_next))
    made = combine(features, row_count, meta, own, squares, got, turn, members)

    heard = jnp.stack([heard, heard_next])
    heard = jnp.concatenate([heard, send(heard, zl_xor=2)])
    aimed_here = heard[..., 0, :] == inst.astype(BF16)
    counts = jnp.sum(
        jnp.where(aimed_here, heard[..., 1, :], jnp.zeros((), BF16))
        .astype(F32)
        .reshape(NZL, NCORE, NX, PAIRS, 2),
        axis=3,
    ).astype(jnp.int32)
    dirty = exchange(made, members, 2)

    counts, *by_x = lax.optimization_barrier((counts, *by_x))
    other_kept = send(jnp.stack([part[:, STORED:] for part in by_x]), dcore=1)
    mig_kv = assemble(
        row_count, meta, counts.reshape(-1), by_x, other_kept, dirty, members
    )
    return decoded, mig_kv


def solution(mesh):
    return jax.shard_map(
        per_device,
        mesh=mesh,
        in_specs=(
            P("inst", None, "tp"),
            P("inst", None, "tp"),
            P("inst", None, "tp"),
            P("inst", None),
            P("inst"),
            P("inst"),
            P("inst"),
            P("inst", None, "tp"),
            P(),
            P(None, "tp"),
        ),
        out_specs=(P("inst", None, "tp"), P("inst", None, "tp")),
        check_vma=False,
    )
```

```python
import functools
import math

import jax
import jax.numpy as jnp
from jax import lax
from jax.experimental import pallas as pl
from jax.experimental.pallas import tpu as pltpu
from jax.sharding import PartitionSpec as P

HD = 128
PAGE = 16
MAXP = 8
MIG = 24
PAIRS = MIG // 2
STORED = MAXP - 2
NX, NZL, NCORE, NZH, NY = 4, 4, 2, 2, 4
TP = NZH * NY
AXES = ("inst", "tp")
F32 = jnp.float32
BF16 = jnp.bfloat16


def index_of(x, zl, core, zh, y):
    return (((x * NZL + zl) * NCORE) + core) * TP + zh * NY + y


def moves(dx=0, dcore=0, dzh=0, dy=0, zl_xor=0):
    pairs = []
    for x in range(NX):
        for zl in range(NZL):
            for core in range(NCORE):
                for zh in range(NZH):
                    for y in range(NY):
                        pairs.append(
                            (
                                index_of(x, zl, core, zh, y),
                                index_of(
                                    (x + dx) % NX,
                                    zl ^ zl_xor,
                                    (core + dcore) % NCORE,
                                    (zh + dzh) % NZH,
                                    (y + dy) % NY,
                                ),
                            )
                        )
    return pairs


def send(value, **by):
    return lax.ppermute(value, AXES, moves(**by))


def params(mebibytes):
    return pltpu.CompilerParams(vmem_limit_bytes=mebibytes * 1024 * 1024)


SMEM = pl.BlockSpec(memory_space=pltpu.SMEM)
VMEM = pl.BlockSpec(memory_space=pltpu.VMEM)
HBM = pl.BlockSpec(memory_space=pltpu.HBM)


def meta_of(table, lengths, rows, target, place):
    parts = [table.reshape(-1), lengths, rows, target, jnp.stack(place)]
    return jnp.concatenate([p.astype(jnp.int32) for p in parts])


def meta_at(row_count):
    lengths = row_count * MAXP
    rows = lengths + row_count
    target = rows + MIG
    return lengths, rows, target, target + MIG


def pack_kernel(row_count, meta_ref, cache_ref, out_ref, held_ref, in_sems, out_sems):
    len_at, rows_at, target_at, place_at = meta_at(row_count)
    x_at, core_at = meta_ref[place_at], meta_ref[place_at + 2]
    for c in range(PAIRS):
        first = meta_ref[rows_at + 2 * c]
        second = meta_ref[rows_at + 2 * c + 1]
        front = (meta_ref[len_at + first] + PAGE - 1) // PAGE - 1
        for m in range(STORED):
            in_front = m < front
            row = jnp.where(in_front, first, second)
            slot = jnp.where(in_front, m, jnp.minimum(m - front, MAXP - 1))
            page = meta_ref[row * MAXP + slot]
            pltpu.make_async_copy(
                cache_ref.at[page], held_ref.at[c, m], in_sems.at[c * STORED + m]
            ).start()

    def out_copy(c):
        target = meta_ref[target_at + 2 * c]
        x, z, core = target // (NZL * NCORE), target // NCORE % NZL, target % NCORE
        far_x = (x - x_at + NX) % NX
        return pltpu.make_async_copy(
            held_ref.at[c],
            out_ref.at[z, far_x, pl.ds((core ^ core_at) * STORED, STORED)],
            out_sems.at[c],
        )

    for c in range(PAIRS):
        for m in range(STORED):
            pltpu.make_async_copy(
                cache_ref.at[0], held_ref.at[c, m], in_sems.at[c * STORED + m]
            ).wait()
        out_copy(c).start()
    for c in range(PAIRS):
        out_copy(c).wait()


def pack(meta, row_count, cache):
    lanes = cache.shape[-1]
    return pl.pallas_call(
        functools.partial(pack_kernel, row_count),
        out_shape=jax.ShapeDtypeStruct(
            (NZL, NX, NCORE * STORED, PAGE, lanes), cache.dtype
        ),
        in_specs=[SMEM, HBM],
        out_specs=HBM,
        scratch_shapes=[
            pltpu.VMEM((PAIRS, STORED, PAGE, lanes), cache.dtype),
            pltpu.SemaphoreType.DMA((PAIRS * STORED,)),
            pltpu.SemaphoreType.DMA((PAIRS,)),
        ],
        compiler_params=params(60),
        cost_estimate=pl.CostEstimate(flops=0, bytes_accessed=4 * 1024 * 1024, transcendentals=0),
        name="pack",
    )(meta, cache)


def attend_kernel(start, row_total, meta_ref, q_ref, new_ref, cache_ref, out_ref):
    row_count, heads, _ = q_ref.shape
    len_at = meta_at(row_total)[0]
    group = 8
    span = MAXP * PAGE + PAGE
    scale = 1.0 / math.sqrt(HD)
    column = lax.broadcasted_iota(jnp.int32, (heads, span), 1)
    step = lax.broadcasted_iota(jnp.int32, (heads, span), 0) // (heads // 2)
    own = (column >= MAXP * PAGE) & (column - MAXP * PAGE <= step)

    def body(i, carry):
        base = i * group
        scores = []
        values = []
        for u in range(group):
            r = base + u
            at = (start + r) * MAXP
            parts = [cache_ref[meta_ref[at + b]] for b in range(MAXP)] + [new_ref[r]]
            tokens = jnp.concatenate(parts, axis=0)
            raw = lax.dot_general(
                q_ref[r], tokens[:, :HD], (((1,), (1,)), ((), ())), preferred_element_type=F32
            )
            seen = (column < meta_ref[len_at + start + r]) | own
            scores.append(jnp.where(seen, raw * scale, -jnp.inf))
            values.append(tokens[:, HD:])
        stacked = jnp.concatenate(scores, axis=0)
        raised = jnp.exp(stacked - jnp.max(stacked, axis=-1, keepdims=True))
        weights = (raised / jnp.sum(raised, axis=-1, keepdims=True)).astype(BF16)
        mixed = [
            jnp.dot(weights[u * heads : (u + 1) * heads], values[u], preferred_element_type=F32)
            for u in range(group)
        ]
        for u in range(group):
            out_ref[base + u] = mixed[u].astype(BF16)
        return carry

    lax.fori_loop(0, row_count // group, body, 0)


def attend(start, row_total, q, fresh, cache, meta):
    row_count, heads, _ = q.shape
    return pl.pallas_call(
        functools.partial(attend_kernel, start, row_total),
        out_shape=jax.ShapeDtypeStruct((row_count, heads, HD), BF16),
        in_specs=[SMEM, VMEM, VMEM, VMEM],
        out_specs=VMEM,
        compiler_params=params(14),
        cost_estimate=pl.CostEstimate(
            flops=row_count * 16 * 144 * 128 * 4,
            bytes_accessed=row_count * 512 * 1024,
            transcendentals=0,
        ),
        name="attend",
    )(meta, q, fresh, cache)


def project_kernel(row_total, meta_ref, gain_ref, own_ref, mine_ref, other_ref, *refs):
    blocks = refs[:5]
    out_own_ref, out_oth_ref, out_sq_ref, in_ref, w_ref, x_ref, sems = refs[5:]
    place_at = meta_at(row_total)[3]
    x_at, core = meta_ref[place_at], meta_ref[place_at + 2]
    zh, y_at = meta_ref[place_at + 3], meta_ref[place_at + 4]
    _, tokens, depth = in_ref.shape
    half = tokens // 2
    part = depth // NCORE
    width = own_ref.shape[1]
    shifts = (0, NY - 1, 1, 2)

    def loads(i):
        y = (y_at + shifts[i]) % NY
        feature = zh * NY + y
        near = (y - x_at + NX) % NX
        rows = [
            pl.ds(pl.multiple_of((core ^ far) * part, part), part) for far in range(NCORE)
        ]
        copies = [
            (
                own_ref.at[pl.ds(pl.multiple_of(feature * depth, depth), depth)],
                w_ref.at[i, :, 0:width],
            ),
            (mine_ref.at[near, 0:part], w_ref.at[i, rows[0], width : 2 * width]),
            (other_ref.at[near, 0:part], w_ref.at[i, rows[1], width : 2 * width]),
        ]
        if i < 3:
            copies.append((blocks[i], in_ref.at[i]))
        else:
            copies.append((blocks[3], in_ref.at[i, 0:half]))
            copies.append((blocks[4], in_ref.at[i, half:tokens]))
        return [
            pltpu.make_async_copy(source, target, sems.at[i, n])
            for n, (source, target) in enumerate(copies)
        ]

    for i in range(NY):
        for copy in loads(i):
            copy.start()
    sums = None
    for i, shift in enumerate(shifts):
        gain = gain_ref[pl.ds(zh * NY + (y_at + shift) % NY, 1), :]
        for copy in loads(i):
            copy.wait()
        states = in_ref[i].astype(F32)
        squares = jnp.broadcast_to(jnp.sum(states * states, axis=1, keepdims=True), (tokens, HD))
        x_ref[i] = (states * gain).astype(BF16)
        parts = (jnp.dot(x_ref[i], w_ref[i], preferred_element_type=F32), squares)
        sums = parts if sums is None else tuple(p + q for p, q in zip(sums, parts))
    products, squares = sums
    out_own_ref[...] = products[:, 0:width]
    out_oth_ref[0:tokens, :] = products[:, width : 2 * width].astype(BF16)
    out_sq_ref[...] = squares
    turned = jnp.transpose(squares)
    front = turned[0:PAGE, 0 : 2 * HD]
    back = jnp.concatenate([turned[0:PAGE, 2 * HD : 3 * HD]] * 2, axis=1)
    line = lax.broadcasted_iota(jnp.int32, (PAGE, 2 * HD), 0)
    value = jnp.where(line < 3, front, back)
    term = line % 3
    high = value.astype(BF16).astype(F32)
    rest = value - high
    middle = rest.astype(BF16).astype(F32)
    lowest = rest - middle
    split = jnp.where(term == 0, high, jnp.where(term == 1, middle, lowest))
    out_oth_ref[tokens : tokens + PAGE, :] = jnp.where(line < 6, split, 0.0).astype(BF16)


def project(row_total, meta, gain, own, mine, other, blocks):
    tokens, depth = blocks[0].shape
    width = own.shape[1]
    return pl.pallas_call(
        functools.partial(project_kernel, row_total),
        out_shape=(
            jax.ShapeDtypeStruct((tokens, width), F32),
            jax.ShapeDtypeStruct((tokens + PAGE, width), BF16),
            jax.ShapeDtypeStruct((tokens, HD), F32),
        ),
        in_specs=[SMEM, VMEM, HBM, HBM, HBM] + [HBM] * len(blocks),
        out_specs=(VMEM, VMEM, VMEM),
        scratch_shapes=[
            pltpu.VMEM((NY, tokens, depth), BF16),
            pltpu.VMEM((NY, depth, 2 * width), BF16),
            pltpu.VMEM((NY, tokens, depth), BF16),
            pltpu.SemaphoreType.DMA((NY, 5)),
        ],
        compiler_params=params(56),
        cost_estimate=pl.CostEstimate(
            flops=NY * tokens * depth * width * 4,
            bytes_accessed=12 * 1024 * 1024,
            transcendentals=0,
        ),
        name="project",
    )(meta, gain, own, mine, other, *blocks)


def combine_kernel(
    features, row_total, meta_ref, own_ref, sq_ref, got_ref, turn_ref, out_ref
):
    tokens = own_ref.shape[0]
    total = own_ref[...] + got_ref[0:tokens, :].astype(F32)
    terms = got_ref[tokens : tokens + PAGE, :].astype(F32)
    line = lax.broadcasted_iota(jnp.int32, terms.shape, 0)
    front = jnp.sum(jnp.where(line < 3, terms, 0.0), axis=0, keepdims=True)
    back = jnp.sum(jnp.where(line >= 3, terms, 0.0), axis=0, keepdims=True)[:, 0:HD]
    row = jnp.concatenate([front, back], axis=1)
    squares = sq_ref[...] + jnp.transpose(jnp.broadcast_to(row, (HD, tokens)))
    inv = lax.rsqrt(squares * (1.0 / features) + 1e-05)
    turn = turn_ref[...]
    other = pltpu.roll(turn, HD // 2, 1)
    in_front = lax.broadcasted_iota(jnp.int32, turn.shape, 1) < HD // 2
    cosine = jnp.where(in_front, turn, other)
    sine = jnp.where(in_front, -other, turn)
    keys = total[:, :HD] * inv
    turned = keys * cosine + pltpu.roll(keys, HD // 2, 1) * sine
    page_rows = jnp.concatenate([turned, total[:, HD:] * inv], axis=1)
    len_at, rows_at, target_at, _ = meta_at(row_total)
    token = lax.broadcasted_iota(jnp.int32, (PAGE, page_rows.shape[1]), 0)
    for k in range(MIG):
        length = meta_ref[len_at + meta_ref[rows_at + k]]
        kept = length - (length - 1) // PAGE * PAGE
        page = jnp.where(token < kept, page_rows[k * PAGE : (k + 1) * PAGE], 0.0)
        out_ref[meta_ref[target_at + k] * 2 + k % 2] = page.astype(BF16)


def combine(features, row_total, meta, own, squares, got, turn, members):
    return pl.pallas_call(
        functools.partial(combine_kernel, features, row_total),
        out_shape=jax.ShapeDtypeStruct((members * 2, PAGE, own.shape[1]), BF16),
        in_specs=[SMEM] + [VMEM] * 4,
        out_specs=VMEM,
        compiler_params=params(10),
        name="combine",
    )(meta, own, squares, got, turn)


def assemble_kernel(row_total, meta_ref, counts_ref, *refs):
    kept_refs, other_ref, dirty_ref, target_ref, out_ref, sems = refs[:NX], *refs[NX:]
    place_at = meta_at(row_total)[3]
    x_at, z_at, core_at = (meta_ref[place_at + i] for i in range(3))

    chunk = NZL * NCORE * MAXP

    def leave(d):
        x = (x_at - d + NX) % NX
        pages = pl.ds(x * chunk, chunk)
        return pltpu.make_async_copy(out_ref.at[pages], target_ref.at[pages], sems.at[d])

    for d in range(NX):
        x = (x_at - d + NX) % NX
        near = (x - x_at + NX) % NX
        for far_core in range(NCORE):

            def one(z, carry, d=d, x=x, near=near, far_core=far_core):
                far_z = z ^ z_at
                source = (x * NZL + z) * NCORE + (core_at ^ far_core)
                entry = (far_z * NCORE + far_core) * NX + near
                first = counts_ref[2 * entry]
                second = counts_ref[2 * entry + 1]
                for m in range(MAXP):
                    behind = (m >= first).astype(jnp.int32)
                    index = jnp.clip(m - behind, 0, STORED - 1)
                    if far_core == 0:
                        kept = kept_refs[d][z, index]
                    else:
                        kept = other_ref[d, z, index]
                    made = dirty_ref[source * 2 + behind]
                    is_made = (m == first - 1) | (m == first + second - 1)
                    page = jnp.where(is_made, made, kept)
                    out_ref[source * MAXP + m] = jnp.where(
                        m < first + second, page, jnp.zeros_like(page)
                    )
                return carry

            lax.fori_loop(0, NZL, one, 0, unroll=2)
        leave(d).start()
    for d in range(NX):
        leave(d).wait()


def assemble(row_total, meta, counts, kept, other, dirty, members):
    lanes = dirty.shape[-1]
    return pl.pallas_call(
        functools.partial(assemble_kernel, row_total),
        out_shape=jax.ShapeDtypeStruct((members * MAXP, PAGE, lanes), dirty.dtype),
        in_specs=[SMEM, SMEM] + [VMEM] * (NX + 2),
        out_specs=HBM,
        scratch_shapes=[
            pltpu.VMEM((members * MAXP, PAGE, lanes), dirty.dtype),
            pltpu.SemaphoreType.DMA((NX,)),
        ],
        compiler_params=params(14),
        name="assemble",
    )(meta, counts, *kept, other, dirty)


def exchange(pages, members, each):
    lanes = pages.shape[-1]
    moved = lax.all_to_all(
        pages.reshape(members, each * PAGE, lanes), "inst", split_axis=0, concat_axis=0, tiled=True
    )
    return moved.reshape(members * each, PAGE, lanes)


def per_device(
    queries,
    new_kv,
    kv_cache,
    block_table,
    lengths,
    mig_rows,
    mig_target,
    dirty_hidden,
    norm_gain,
    kv_weight,
):
    members = lax.axis_size("inst")
    inst = lax.axis_index("inst")
    tp = lax.axis_index("tp")
    x_at, z_lo, core = inst // (NZL * NCORE), inst // NCORE % NZL, inst % NCORE
    zh, y_at = tp // NY, tp % NY
    tokens = MIG * PAGE
    depth = dirty_hidden.shape[-1]
    features = depth * TP
    half_features = depth * NY

    row_count = queries.shape[0]
    meta = meta_of(block_table, lengths, mig_rows, mig_target, (x_at, z_lo, core, zh, y_at))

    hidden = dirty_hidden.reshape(tokens, depth)
    from_below = send(hidden, dy=1)
    from_above = send(hidden, dy=-1)

    picked = mig_rows[:, None] == jnp.arange(row_count, dtype=jnp.int32)[None, :]
    mig_len = jnp.sum(jnp.where(picked, lengths[None, :], 0), axis=1)
    mig_pages = (mig_len + PAGE - 1) // PAGE

    slice_rows = half_features // (NX * NCORE)
    begin = (1 - zh) * half_features + (x_at * NCORE + core) * slice_rows
    width = kv_weight.shape[1]
    slice_here = send(
        lax.dynamic_slice_in_dim(kv_weight, begin, slice_rows, axis=0), dzh=1, zl_xor=2
    )
    notes = jnp.pad(
        jnp.stack([mig_target, mig_pages]).astype(BF16), ((0, PAGE - 2), (0, width - MIG))
    )
    packed = pack(meta, row_count, kv_cache)
    slice_here, from_below, from_above, _ = lax.optimization_barrier(
        (slice_here, from_below, from_above, packed)
    )
    noted = jnp.concatenate([slice_here, notes], axis=0)
    across_top = send(from_below[: tokens // 2], dy=1)
    across_bottom = send(from_above[tokens // 2 :], dy=-1)
    slices = jnp.stack([noted] + [send(noted, dx=-d) for d in range(1, NX)])

    lines = [
        [(x * NZL + z) * NCORE + c for z in range(NZL)] for x in range(NX) for c in range(NCORE)
    ]
    by_z = lax.all_to_all(
        packed, "inst", split_axis=0, concat_axis=0, axis_index_groups=lines, tiled=True
    )

    offsets = jnp.arange(PAGE, dtype=jnp.int32)
    positions = ((mig_pages - 1) * PAGE)[:, None] + offsets[None, :]
    half_dim = HD // 2
    frequency = jnp.exp(
        jnp.arange(half_dim, dtype=F32) * (-2.0 * math.log(500000.0) / HD)
    )
    angles = positions.reshape(tokens).astype(F32)[:, None] * frequency[None, :]
    turn = jnp.concatenate([jnp.cos(angles), jnp.sin(angles)], axis=1)

    gain = norm_gain.astype(F32).reshape(TP, depth)

    slices, across_top, across_bottom = lax.optimization_barrier(
        (slices, across_top, across_bottom)
    )
    other_slices = send(slices, dcore=1)
    own, outgoing, squares = project(
        row_count,
        meta,
        gain,
        kv_weight,
        slices,
        other_slices,
        (hidden, from_below, from_above, across_top, across_bottom),
    )
    got = send(outgoing, dzh=1)

    heads = queries.shape[-1] // HD
    q = queries.reshape(row_count, 2 * heads, HD)
    fresh = jnp.pad(new_kv, ((0, 0), (0, PAGE - 2), (0, 0)))
    q, fresh, _ = lax.optimization_barrier((q, fresh, outgoing))
    decoded = attend(0, row_count, q, fresh, kv_cache, meta)
    decoded = decoded.reshape(row_count, 2, heads * HD)
    by_z, decoded = lax.optimization_barrier((by_z, decoded))
    lines = slice(slice_rows, slice_rows + 2)
    heard = jnp.stack([slices[:, lines, :MIG], other_slices[:, lines, :MIG]])
    heard, _ = lax.optimization_barrier((heard, outgoing))
    heard_next = send(heard, zl_xor=1)
    by_x = [by_z[:, d] for d in range(NX)]
    got, *by_x[1:] = lax.optimization_barrier((got, *by_x[1:]))
    by_x = [by_x[0]] + [send(by_x[d], dx=d) for d in range(1, NX)]
    got, turn, heard_next = lax.optimization_barrier((got, turn, heard_next))
    made = combine(features, row_count, meta, own, squares, got, turn, members)

    heard = jnp.stack([heard, heard_next])
    heard = jnp.concatenate([heard, send(heard, zl_xor=2)])
    aimed_here = heard[..., 0, :] == inst.astype(BF16)
    counts = jnp.sum(
        jnp.where(aimed_here, heard[..., 1, :], jnp.zeros((), BF16))
        .astype(F32)
        .reshape(NZL, NCORE, NX, PAIRS, 2),
        axis=3,
    ).astype(jnp.int32)
    dirty = exchange(made, members, 2)

    counts, *by_x = lax.optimization_barrier((counts, *by_x))
    other_kept = send(jnp.stack([part[:, STORED:] for part in by_x]), dcore=1)
    mig_kv = assemble(
        row_count, meta, counts.reshape(-1), by_x, other_kept, dirty, members
    )
    return decoded, mig_kv


def solution(mesh):
    return jax.shard_map(
        per_device,
        mesh=mesh,
        in_specs=(
            P("inst", None, "tp"),
            P("inst", None, "tp"),
            P("inst", None, "tp"),
            P("inst", None),
            P("inst"),
            P("inst"),
            P("inst"),
            P("inst", None, "tp"),
            P(),
            P(None, "tp"),
        ),
        out_specs=(P("inst", None, "tp"), P("inst", None, "tp")),
        check_vma=False,
    )
```
